32 devices in a mesh: sample: 4 (over z), landmark: 8 (over y, x, core).
Axes of the slice: x: 2, y: 2, z: 4, core: 2. Of those that a mesh axis runs over, the one named last changes fastest.
Arguments:
- embeddings: bfloat16 [4096, 4096], P('sample'), may hold values from -6 to 6
- landmarks: bfloat16 [16384, 4096], P('landmark'), may hold values from -6 to 6
- factor: bfloat16 [16384, 16384], P('landmark', 'sample')
- flips: int32 [512, 4096], P(None, 'sample'), may hold values from 0 to 1
- labels: int32 [4096], P('sample'), may hold values from 0 to 1, as said below
- counts: int32 [4], replicated, may hold values from 256 to 1024, as said below
Outputs:
- whitened: bfloat16 [16384, 512], P(('sample', 'landmark'))
- statistic: float32 [512], replicated
The draws below stay inside these ranges and needn't reach their ends.
Inputs may be any that keep to these rules, and one draw needn't show every extreme that they name: `counts`: one slab holds exactly 1024 live rows. `labels`: 0 or 1; the first slot of every slab is of corpus 0 and the second of corpus 1.
All inputs are finite; a program needn't handle non-finite values.
Results may differ from the reference program's by a relative error of at most 0.029.
Values may be sent and summed in bfloat16 or wider, within the bound.
No kernel may reach another device: no remote copies, remote signals or barrier semaphores. Data moves between devices by JAX's collectives and lax.ppermute only.
A program may use at most 128 MiB of HBM per device.

```python
import math
import jax
import jax.numpy as jnp
from jax import lax

D = 4096
LANDMARKS = 16384
PERMS = 512
ROWS_DEV = 1024
ROWS = 4096
N_SAMPLE = 4
N_LANDMARK = 8


def draw_factor(key, part):
    entry_key = jax.random.fold_in(key, 11)
    scale_key = jax.random.fold_in(key, 12)
    entries = jnp.clip(jax.random.normal(entry_key, (LANDMARKS, LANDMARKS), jnp.float32), -5.0, 5.0)
    logs = jax.random.uniform(scale_key, (1, LANDMARKS), jnp.float32, -1.204, 1.099)
    values = entries * jnp.exp(logs) * (1.0 / jnp.sqrt(jnp.float32(LANDMARKS)))
    return values.astype(jnp.bfloat16)


def draw_labels(key, part):
    slabs = ROWS // ROWS_DEV
    side = jax.random.randint(jax.random.fold_in(key, 22), (), 0, 2, dtype=jnp.int32)
    base = jax.random.randint(jax.random.fold_in(key, 23), (), 20, 36, dtype=jnp.int32)
    share = jnp.where(side == 0, base, 100 - base)
    jitter = jax.random.randint(jax.random.fold_in(key, 24), (slabs,), -10, 11, dtype=jnp.int32)
    threshold = share + jitter
    slab_of = jnp.arange(ROWS, dtype=jnp.int32) // ROWS_DEV
    row_threshold = jnp.sum(jnp.where(slab_of[:, None] == jnp.arange(slabs, dtype=jnp.int32)[None, :], threshold[None, :], 0), axis=1)
    draws = jax.random.randint(jax.random.fold_in(key, 21), (ROWS,), 0, 100, dtype=jnp.int32)
    bits = jnp.where(draws < row_threshold, 1, 0)
    slot = jnp.arange(ROWS, dtype=jnp.int32) % ROWS_DEV
    bits = jnp.where(slot == 0, 0, bits)
    bits = jnp.where(slot == 1, 1, bits)
    return bits.astype(jnp.int32)


def draw_counts(key, part):
    slabs = ROWS // ROWS_DEV
    base = jax.random.randint(jax.random.fold_in(key, 31), (slabs,), ROWS_DEV // 4, ROWS_DEV + 1, dtype=jnp.int32)
    chosen = jax.random.randint(jax.random.fold_in(key, 32), (), 0, slabs, dtype=jnp.int32)
    return jnp.where(jnp.arange(slabs, dtype=jnp.int32) == chosen, ROWS_DEV, base).astype(jnp.int32)


def with_ends(drawn, own_key, smallest, high):
    spot = [jax.random.randint(jax.random.fold_in(own_key, axis), (), 0, length) for axis, length in enumerate(drawn.shape)]
    main_axis = drawn.shape.index(max(drawn.shape))
    beside = spot[:main_axis] + [(spot[main_axis] + 1) % drawn.shape[main_axis]] + spot[main_axis + 1:]
    return drawn.at[tuple(spot)].set(smallest).at[tuple(beside)].set(high)


def block_scale(own_key, shape, shards, smallest, top_value):
    def one(position, shards_of):
        heights = jax.random.uniform(jax.random.fold_in(jax.random.fold_in(own_key, 6), position), (shards_of,), jnp.float32, smallest / len(shards), top_value / len(shards))
        return jnp.repeat(jnp.exp(heights), shape[position] // shards_of).reshape((-1,) + (1,) * (len(shape) - position - 1))

    level = one(*shards[0])
    for cut in shards[1:]:
        level = level * one(*cut)
    return level


def normal_values(key, dims, spread, reach, shards=(), held_as=jnp.bfloat16):
    loudness = block_scale(key, dims, shards, -0.22, 0.18) if shards else 1.0
    drawn = jax.random.normal(key, dims, jnp.float32) * spread * loudness
    return jnp.minimum(jnp.maximum(drawn, -reach), reach).astype(held_as)


def setup_inputs(seed: int = 0) -> dict:
    key_of = jax.random.split(jax.random.key(seed), 7)
    embeddings = normal_values(key_of[0], (ROWS, D), 1.0, 6.0, ((0, 4),))
    landmarks = normal_values(key_of[1], (LANDMARKS, D), 1.0, 6.0, ((0, 8),))
    factor = draw_factor(jax.random.fold_in(key_of[6], 71), 0)
    flips = with_ends(jax.random.randint(key_of[3], (PERMS, ROWS), 0, 2), jax.random.fold_in(key_of[3], 1), 0, 1).astype(jnp.int32)
    labels = draw_labels(jax.random.fold_in(key_of[6], 71), 0)
    counts = draw_counts(jax.random.fold_in(key_of[6], 71), 0)
    return {"embeddings": embeddings, "landmarks": landmarks, "factor": factor, "flips": flips, "labels": labels, "counts": counts}


def reference(embeddings, landmarks, factor, flips, labels, counts):
    total_rows = embeddings.shape[0]
    slot_index = jnp.arange(total_rows, dtype=jnp.int32)
    slab_index = slot_index // ROWS_DEV
    live_rows = (slot_index % ROWS_DEV < counts[slab_index]).astype(jnp.float32)
    corpus = labels.astype(jnp.float32)
    count_a = jnp.sum(live_rows * (1.0 - corpus))
    count_b = jnp.sum(live_rows * corpus)
    balance = jnp.sqrt(count_a * count_b / (count_a + count_b))
    row_weight = live_rows * ((1.0 - corpus) / count_a - corpus / count_b) * balance
    wide_x = embeddings.astype(jnp.float32)
    row_scale = lax.rsqrt(lax.optimization_barrier(jnp.mean(wide_x * wide_x, axis=1)) + 1e-06)
    signs = (2 * flips - 1).astype(jnp.bfloat16)
    slab_signs = signs.reshape(PERMS, N_SAMPLE, ROWS_DEV).astype(jnp.float32)
    block_size = LANDMARKS // N_LANDMARK

    def kernel_block(points):
        wide_z = points.astype(jnp.float32)
        point_scale = lax.rsqrt(lax.optimization_barrier(jnp.mean(wide_z * wide_z, axis=1)) + 1e-06)
        cross = lax.dot_general(embeddings, points, (((1,), (1,)), ((), ())), preferred_element_type=jnp.float32)
        kern = jnp.exp(0.5 * cross * row_scale[:, None] * point_scale[None, :] / math.sqrt(D))
        weighted = (row_weight[:, None] * kern).astype(jnp.bfloat16)
        slab_weighted = weighted.reshape(N_SAMPLE, ROWS_DEV, block_size).astype(jnp.float32)
        slab_moments = jnp.einsum('psr,srl->spl', slab_signs, slab_weighted).astype(jnp.bfloat16)
        slab_moments = lax.optimization_barrier(slab_moments)
        return lax.optimization_barrier(jnp.sum(slab_moments.astype(jnp.float32), axis=0)).astype(jnp.bfloat16)
    blocks = landmarks.reshape(N_LANDMARK, block_size, D)
    moments = lax.map(kernel_block, blocks)
    moments = jnp.transpose(moments, (1, 0, 2)).reshape(PERMS, LANDMARKS)
    wide = lax.dot_general(factor, moments, (((0,), (1,)), ((), ())), preferred_element_type=jnp.float32)
    statistic = lax.optimization_barrier(jnp.sum(wide * wide, axis=0)) / LANDMARKS
    return (wide.astype(jnp.bfloat16), statistic)
```

```python
import functools
import math

import jax
import jax.numpy as jnp
from jax import lax
from jax.experimental import pallas as pl
from jax.experimental.pallas import tpu as pltpu
from jax.sharding import PartitionSpec as P

VMEM_LIMIT = 40 * 1024 * 1024
L_CHUNKS = 4
P_SPLIT = 2
NT = (((1,), (1,)), ((), ()))


def row_stats_kernel(x_ref, flips_ref, scale_ref, signs_ref):
    x = x_ref[...].astype(jnp.float32)
    mean = jnp.sum(x * x, axis=1, keepdims=True) * (1.0 / x.shape[1])
    scale_ref[...] = lax.rsqrt(mean + 1e-06) * (0.5 / math.sqrt(x.shape[1]))
    signs_ref[...] = (2 * flips_ref[...] - 1).astype(jnp.bfloat16)


def row_stats(x, flips):
    rows, width = x.shape
    perms = flips.shape[0]
    steps = 8
    return pl.pallas_call(
        row_stats_kernel,
        grid=(steps,),
        in_specs=[
            pl.BlockSpec((rows // steps, width), lambda i: (i, 0)),
            pl.BlockSpec((perms // steps, rows), lambda i: (i, 0)),
        ],
        out_specs=[
            pl.BlockSpec((rows // steps, 1), lambda i: (i, 0)),
            pl.BlockSpec((perms // steps, rows), lambda i: (i, 0)),
        ],
        out_shape=[
            jax.ShapeDtypeStruct((rows, 1), jnp.float32),
            jax.ShapeDtypeStruct((perms, rows), jnp.bfloat16),
        ],
        compiler_params=pltpu.CompilerParams(vmem_limit_bytes=VMEM_LIMIT),
        cost_estimate=pl.CostEstimate(flops=2 * rows * width, bytes_accessed=rows * width * 2, transcendentals=0),
        name="row_stats",
    )(x, flips)


def moments_kernel(x_ref, z_ref, scale_ref, weight_ref, signs_ref, *outs):
    rows = x_ref.shape[0]
    z = z_ref[...]
    z32 = z.astype(jnp.float32)
    mean = jnp.sum(z32 * z32, axis=1, keepdims=True) * (1.0 / z.shape[1])
    point = jnp.broadcast_to(lax.rsqrt(mean + 1e-06), (z.shape[0], 128))
    point_row = jnp.transpose(point)[0:1, :]
    parts = []
    block = 256
    for r in range(0, rows, block):
        here = pl.ds(r, block)
        cross = lax.dot_general(x_ref[here, :], z, NT, preferred_element_type=jnp.float32)
        kern = jnp.exp(cross * scale_ref[here, :] * point_row)
        parts.append((weight_ref[here, :] * kern).astype(jnp.bfloat16))
    weighted = jnp.concatenate(parts, axis=0)
    at = 0
    for out in outs:
        here = pl.ds(at, out.shape[0])
        out[...] = jnp.dot(signs_ref[here, :], weighted, preferred_element_type=jnp.float32).astype(jnp.bfloat16)
        at += out.shape[0]


def moments_part(x, z, scale, weight, signs, first, count, sizes):
    rows, width = x.shape
    tile = 256
    per = count // tile
    perms = signs.shape[0]
    return pl.pallas_call(
        moments_kernel,
        grid=(per,),
        in_specs=[
            pl.BlockSpec((rows, width), lambda i: (0, 0)),
            pl.BlockSpec((tile, width), lambda i: (first // tile + i, 0)),
            pl.BlockSpec((rows, 1), lambda i: (0, 0)),
            pl.BlockSpec((rows, 1), lambda i: (0, 0)),
            pl.BlockSpec((perms, rows), lambda i: (0, 0)),
        ],
        out_specs=[pl.BlockSpec((size, tile), lambda i: (0, i)) for size in sizes],
        out_shape=[jax.ShapeDtypeStruct((size, count), jnp.bfloat16) for size in sizes],
        compiler_params=pltpu.CompilerParams(vmem_limit_bytes=VMEM_LIMIT),
        cost_estimate=pl.CostEstimate(
            flops=2 * rows * width * count + 2 * perms * rows * count,
            bytes_accessed=(rows + count) * width * 2,
            transcendentals=rows * count,
        ),
        name="moments",
    )(x, z, scale, weight, signs)


def whiten_kernel(table_ref, factor_ref, *refs):
    out = refs[-1]
    depth = refs[0].shape[1]
    total = None
    for i, part in enumerate(refs[:-1]):
        term = jnp.dot(part[...], factor_ref[pl.ds(i * depth, depth), :], preferred_element_type=jnp.float32)
        total = term if total is None else total + term
    out[0] = total.astype(jnp.bfloat16)


def whiten(table, factor, parts, blocks):
    depth, columns = factor.shape
    perms, piece = parts[0].shape
    count = table.shape[0]
    wide = columns // blocks
    return pl.pallas_call(
        whiten_kernel,
        grid_spec=pltpu.PrefetchScalarGridSpec(
            num_scalar_prefetch=1,
            grid=(count,),
            in_specs=[pl.BlockSpec((depth, wide), lambda i, t: (0, t[i]))]
            + [pl.BlockSpec((perms, piece), lambda i, t: (0, 0)) for _ in parts],
            out_specs=pl.BlockSpec((1, perms, wide), lambda i, t: (i, 0, 0)),
        ),
        out_shape=jax.ShapeDtypeStruct((count, perms, wide), jnp.bfloat16),
        compiler_params=pltpu.CompilerParams(vmem_limit_bytes=VMEM_LIMIT),
        cost_estimate=pl.CostEstimate(
            flops=2 * perms * depth * wide * count,
            bytes_accessed=depth * wide * count * 2,
            transcendentals=0,
        ),
        name="whiten",
    )(table, factor, *parts)


def finish_kernel(*refs):
    half = (len(refs) - 2) // 2
    out, share = refs[-2:]
    at = 0
    for i in range(half):
        a = refs[2 * i][...].astype(jnp.float32) + refs[2 * i + 1][...].astype(jnp.float32)
        here = pl.ds(at, a.shape[0])
        wide = jnp.transpose(a)
        out[:, here] = wide.astype(jnp.bfloat16)
        share[:, here] = jnp.broadcast_to(jnp.sum(wide * wide, axis=0, keepdims=True), (8, a.shape[0]))
        at += a.shape[0]


def finish(pairs):
    flat = [a for pair in pairs for a in pair]
    perms = sum(pair[0].shape[0] for pair in pairs)
    wide = flat[0].shape[1]
    return pl.pallas_call(
        finish_kernel,
        out_shape=[
            jax.ShapeDtypeStruct((wide, perms), jnp.bfloat16),
            jax.ShapeDtypeStruct((8, perms), jnp.float32),
        ],
        compiler_params=pltpu.CompilerParams(vmem_limit_bytes=VMEM_LIMIT),
        cost_estimate=pl.CostEstimate(flops=4 * perms * wide, bytes_accessed=perms * wide * 6, transcendentals=0),
        name="finish",
    )(*flat)


def pick(options, here):
    items = sorted(options.items())
    value = items[0][1]
    for position, array in items[1:]:
        value = jnp.where(here == position, array, value)
    return value


class Chain:
    def __init__(self, size, here, pieces):
        self.size, self.here, self.pieces = size, here, pieces
        self.right, self.left = [], []

    def steps(self):
        return len(self.pieces) + self.size - 2

    def _send(self, t, recv, mirror):
        n, count = self.size, len(self.pieces)
        options = {}
        for r in range(n - 1):
            if 0 <= t - r < count:
                options[n - 1 - r if mirror else r] = self.pieces[t - r]
        own = pick(options, self.here)
        if t > 0:
            own = (own.astype(jnp.float32) + recv[t - 1].astype(jnp.float32)).astype(jnp.bfloat16)
        return own

    def step(self, t):
        n = self.size
        to_right = self._send(t, self.right, False)
        to_left = self._send(t, self.left, True)
        self.right.append(lax.ppermute(to_right, "sample", [(i, i + 1) for i in range(n - 1)]))
        self.left.append(lax.ppermute(to_left, "sample", [(i + 1, i) for i in range(n - 1)]))

    def total(self, i):
        n = self.size
        total = self.pieces[i].astype(jnp.float32)
        from_left = {z: self.right[i + z - 1] for z in range(1, n)}
        from_right = {z: self.left[i + n - 2 - z] for z in range(n - 1)}
        total = total + pick(from_left, self.here).astype(jnp.float32)
        total = total + pick(from_right, self.here).astype(jnp.float32)
        return total.astype(jnp.bfloat16)


def exchange_sum(value, axis, size):
    total = value
    for shift in range(1, size):
        total = total + lax.ppermute(value, axis, [(i, (i + shift) % size) for i in range(size)])
    return total


def make_local(mesh):
    n_sample = mesh.shape["sample"]
    n_landmark = mesh.shape["landmark"]
    bits = n_landmark.bit_length() - 1

    def order_of(core):
        rest = list(range(1, bits))
        return [0] + (rest if core == 0 else rest[::-1])

    def place_of(core, q):
        return sum(((q >> t) & 1) << bit for t, bit in enumerate(order_of(core)))

    def local(embeddings, landmarks, factor, flips, labels, counts):
        slot_count = embeddings.shape[0]
        slab_total = counts.shape[0]
        here = lax.axis_index("sample")
        spot = lax.axis_index("landmark")
        own_count = jnp.sum(jnp.where(jnp.arange(slab_total, dtype=jnp.int32) == here, counts, 0))
        live_rows = (jnp.arange(slot_count, dtype=jnp.int32) < own_count).astype(jnp.float32)
        corpus = labels.astype(jnp.float32)
        own_pair = jnp.stack([jnp.sum(live_rows * (1.0 - corpus)), jnp.sum(live_rows * corpus)])
        pair = exchange_sum(own_pair, "sample", n_sample)
        count_a, count_b = pair[0], pair[1]
        balance = jnp.sqrt(count_a * count_b / (count_a + count_b))
        row_weight = live_rows * ((1.0 - corpus) / count_a - corpus / count_b) * balance
        row_weight = row_weight[:, None]
        row_scale, signs = row_stats(embeddings, flips)

        perms = flips.shape[0]
        points = landmarks.shape[0]
        chunk = points // L_CHUNKS
        sizes = [perms // P_SPLIT] * P_SPLIT
        chains = [Chain(n_sample, here, []) for _ in sizes]
        for k in range(L_CHUNKS):
            outs = moments_part(embeddings, landmarks, row_scale, row_weight, signs, k * chunk, chunk, sizes)
            for chain, out in zip(chains, outs):
                chain.pieces.append(out)

        core = spot % 2
        half = n_landmark // 2
        sent_places = [1 + 2 * q for q in range(half)]
        kept_places = [2 * q for q in range(half)]

        def table_of(places, order_core):
            zero = jnp.array([place_of(0, q) for q in places], jnp.int32)
            one = jnp.array([place_of(1, q) for q in places], jnp.int32)
            return jnp.bitwise_xor(jnp.where(order_core == 0, zero, one), spot.astype(jnp.int32))

        kept_order = sorted(kept_places, key=lambda q: [-((q >> t) & 1) for t in range(1, bits)])
        sent_order = [q + 1 for q in kept_order]
        kept_table = table_of(kept_order, core)
        sent_table = table_of(sent_order, 1 - core)

        def pairs_of(t):
            return [(m, m ^ (1 << order_of(m % 2)[t])) for m in range(n_landmark)]

        pairs = []
        for chain in chains:
            for t in range(chain.steps()):
                chain.step(t)
            totals = [chain.total(i) for i in range(len(chain.pieces))]
            sent = whiten(sent_table, factor, totals, n_landmark)
            recv = lax.ppermute(sent, "landmark", pairs_of(0))
            kept = whiten(kept_table, factor, totals, n_landmark)
            for t in range(1, bits):
                middle = kept.shape[0] // 2
                both = lambda a, b: (a.astype(jnp.float32) + b.astype(jnp.float32)).astype(jnp.bfloat16)
                sent = both(kept[:middle], recv[:middle])
                kept = both(kept[middle:], recv[middle:])
                recv = lax.ppermute(sent, "landmark", pairs_of(t))
            pairs.append((kept[0], recv[0]))
        whitened, share = finish(pairs)
        share = exchange_sum(share[0], "landmark", n_landmark)
        share = exchange_sum(share, "sample", n_sample)
        total_points = points * n_landmark
        return whitened, share / total_points

    return local


def solution(mesh):
    return jax.shard_map(
        make_local(mesh),
        mesh=mesh,
        in_specs=(
            P("sample", None),
            P("landmark", None),
            P("landmark", "sample"),
            P(None, "sample"),
            P("sample"),
            P(),
        ),
        out_specs=(P(("sample", "landmark"), None), P()),
        check_vma=False,
    )
```

```python
import functools
import math

import jax
import jax.numpy as jnp
from jax import lax
from jax.experimental import pallas as pl
from jax.experimental.pallas import tpu as pltpu
from jax.sharding import PartitionSpec as P

VMEM_LIMIT = 14 * 1024 * 1024
TILE = 256
NT = (((1,), (1,)), ((), ()))


VMEM = pl.BlockSpec(memory_space=pltpu.VMEM)
SMEM = pl.BlockSpec(memory_space=pltpu.SMEM)
HBM = pl.BlockSpec(memory_space=pltpu.HBM)
ANY = pl.BlockSpec(memory_space=pl.ANY)


def in_hbm(x):
    return pltpu.with_memory_space_constraint(x, pltpu.HBM)


def call(kernel, name, out_shape, in_specs, args, flops=0, bytes_accessed=0, transcendentals=0, scratch=()):
    return pl.pallas_call(
        kernel,
        out_shape=out_shape,
        in_specs=in_specs,
        out_specs=jax.tree.map(lambda _: VMEM, out_shape),
        scratch_shapes=list(scratch),
        compiler_params=pltpu.CompilerParams(vmem_limit_bytes=VMEM_LIMIT),
        cost_estimate=pl.CostEstimate(
            flops=flops, bytes_accessed=bytes_accessed, transcendentals=transcendentals
        ),
        name=name,
    )(*args)


def slot_masks(labels, own_count, slots):
    live = slots < own_count
    return (live & (labels == 0)).astype(jnp.float32), (live & (labels != 0)).astype(jnp.float32)


def counts_kernel(here_ref, counts_ref, labels_ref, out_ref):
    own_count = counts_ref[here_ref[0]]
    shape = labels_ref.shape
    slots = lax.broadcasted_iota(jnp.int32, shape, 0) * shape[1] + lax.broadcasted_iota(jnp.int32, shape, 1)
    mask_a, mask_b = slot_masks(labels_ref[...], own_count, slots)
    first = lax.broadcasted_iota(jnp.int32, out_ref.shape[1:], 0) == 0
    pair = jnp.where(first, jnp.sum(mask_a), jnp.sum(mask_b))
    out_ref[...] = jnp.broadcast_to(pair[None], out_ref.shape)


def own_counts(here, counts, labels, copies):
    return call(
        counts_kernel,
        "own_counts",
        jax.ShapeDtypeStruct((copies, 8, 128), jnp.float32),
        [SMEM, SMEM, VMEM],
        (here, counts, labels.reshape(-1, 128)),
    )


def rows_kernel(parts, here_ref, counts_ref, x_ref, z_ref, flips_ref, labels_ref,
                held_ref, first_ref, scale_ref, signs_ref, mask_a_ref, mask_b_ref, flips_buf, x_sem, z_sem, f_sem):
    rows, width = x_ref.shape
    block = rows // parts

    def x_copy(i):
        here = pl.ds(i * block, block)
        return pltpu.make_async_copy(x_ref.at[here, :], held_ref.at[here, :], x_sem.at[i])

    flips_copy = pltpu.make_async_copy(flips_ref, flips_buf, f_sem)
    z_copy = pltpu.make_async_copy(z_ref.at[pl.ds(0, first_ref.shape[0]), :], first_ref, z_sem)
    for i in range(parts):
        x_copy(i).start()
    z_copy.start()
    flips_copy.start()
    own_count = counts_ref[here_ref[0]]
    for j in range(rows // 128):
        here = pl.ds(j * 128, 128)
        labels = jnp.transpose(jnp.broadcast_to(labels_ref[pl.ds(j, 1), :], (128, 128)))[:, 0:1]
        slots = j * 128 + lax.broadcasted_iota(jnp.int32, (128, 1), 0)
        mask_a_ref[here, :], mask_b_ref[here, :] = slot_masks(labels, own_count, slots)
    for i in range(parts):
        x_copy(i).wait()
        here = pl.ds(i * block, block)
        x = held_ref[here, :].astype(jnp.float32)
        mean = jnp.sum(x * x, axis=1, keepdims=True) * (1.0 / width)
        scale_ref[here, :] = lax.rsqrt(mean + 1e-06) * (0.5 / math.sqrt(width))
    flips_copy.wait()
    signs_ref[...] = (2 * flips_buf[...] - 1).astype(jnp.bfloat16)
    z_copy.wait()


def prepare_rows(here, counts, x, z, flips, labels):
    rows, width = x.shape
    perms = flips.shape[0]
    parts = 8
    column = jax.ShapeDtypeStruct((rows, 1), jnp.float32)
    return call(
        functools.partial(rows_kernel, parts),
        "prepare_rows",
        [
            pltpu.VMEM((rows, width), x.dtype),
            jax.ShapeDtypeStruct((TILE, width), z.dtype),
            column,
            jax.ShapeDtypeStruct((perms, rows), jnp.bfloat16),
            column,
            column,
        ],
        [SMEM, SMEM, HBM, HBM, HBM, VMEM],
        (here, counts, in_hbm(x), in_hbm(z), in_hbm(flips), labels.reshape(-1, 128)),
        flops=3 * rows * width,
        bytes_accessed=(rows + TILE) * width * 2 + perms * rows * 4,
        scratch=[
            pltpu.VMEM(flips.shape, flips.dtype),
            pltpu.SemaphoreType.DMA((parts,)),
            pltpu.SemaphoreType.DMA,
            pltpu.SemaphoreType.DMA,
        ],
    )


def moments_kernel(following, after, pair_ref, x_ref, z_ref, scale_ref, signs_ref, mask_a_ref, mask_b_ref, z_all_ref,
                   *rest):
    out_ref, *rest = rest[after:]
    rows, width = x_ref.shape
    if following is not None:
        next_ref, sem = rest
        next_copy = pltpu.make_async_copy(z_all_ref.at[pl.ds(following, TILE), :], next_ref, sem)
        next_copy.start()
    pair = jnp.sum(pair_ref[...], axis=0)
    count_a, count_b = pair[0:1, 0:1], pair[1:2, 0:1]
    balance = jnp.sqrt(count_a * count_b / (count_a + count_b))
    weight_a, weight_b = balance / count_a, balance / count_b
    z = z_ref[...]
    z32 = z.astype(jnp.float32)
    mean = jnp.sum(z32 * z32, axis=1, keepdims=True) * (1.0 / width)
    point = jnp.broadcast_to(lax.rsqrt(mean + 1e-06), (TILE, 128))
    point_row = jnp.transpose(point)[0:1, :]
    cross = lax.dot_general(x_ref[...], z, NT, preferred_element_type=jnp.float32)
    kern = jnp.exp(cross * scale_ref[...] * point_row)
    weight = mask_a_ref[...] * weight_a - mask_b_ref[...] * weight_b
    weighted = (weight * kern).astype(jnp.bfloat16)
    out_ref[...] = jnp.dot(signs_ref[...], weighted, preferred_element_type=jnp.float32).astype(jnp.bfloat16)
    if following is not None:
        next_copy.wait()


def moments_part(pair, x, z, scale, signs, mask_a, mask_b, z_all, following, after):
    rows, width = x.shape
    perms = signs.shape[0]
    out_shape = [jax.ShapeDtypeStruct((perms, TILE), jnp.bfloat16)]
    scratch = []
    if following is not None:
        out_shape.append(jax.ShapeDtypeStruct((TILE, width), z.dtype))
        scratch.append(pltpu.SemaphoreType.DMA)
    return call(
        functools.partial(moments_kernel, following, len(after)),
        "moments",
        out_shape,
        [VMEM] * 7 + [HBM] + [ANY] * len(after),
        (pair, x, z, scale, signs, mask_a, mask_b, in_hbm(z_all), *after),
        flops=2 * rows * width * TILE + 2 * perms * rows * TILE,
        bytes_accessed=TILE * width * 2,
        transcendentals=rows * TILE,
        scratch=scratch,
    )


def whiten_kernel(table_ref, factor_ref, *refs):
    out = refs[-1]
    moments = jnp.concatenate([part[...] for part in refs[:-1]], axis=1)
    wide = out.shape[2]
    for i in range(out.shape[0]):
        here = pl.ds(pl.multiple_of(table_ref[i] * wide, wide), wide)
        out[i] = jnp.dot(moments, factor_ref[:, here], preferred_element_type=jnp.float32).astype(jnp.bfloat16)


def whiten(table, factor, parts, blocks):
    depth, columns = factor.shape
    perms = parts[0].shape[0]
    count = table.shape[0]
    wide = columns // blocks
    return call(
        whiten_kernel,
        "whiten",
        jax.ShapeDtypeStruct((count, perms, wide), jnp.bfloat16),
        [SMEM] + [VMEM] * (1 + len(parts)),
        (table, factor, *parts),
        flops=2 * perms * depth * wide * count,
        bytes_accessed=depth * wide * count * 2,
    )


def finish_kernel(a_ref, b_ref, out_ref, share_ref):
    wide = jnp.transpose(a_ref[...].astype(jnp.float32) + b_ref[...].astype(jnp.float32))
    out_ref[...] = wide.astype(jnp.bfloat16)
    share = jnp.sum(wide * wide, axis=0, keepdims=True)
    for j in range(share_ref.shape[1]):
        row = share[:, j * 128:(j + 1) * 128]
        share_ref[:, j, :] = jnp.broadcast_to(row, (share_ref.shape[0], 128))


def finish(a, b, copies):
    perms, wide = a.shape
    return call(
        finish_kernel,
        "finish",
        [
            jax.ShapeDtypeStruct((wide, perms), jnp.bfloat16),
            jax.ShapeDtypeStruct((copies, perms // 128, 128), jnp.float32),
        ],
        [VMEM, VMEM],
        (a, b),
        flops=4 * perms * wide,
        bytes_accessed=perms * wide * 6,
    )


def add(a, b):
    return (a.astype(jnp.float32) + b.astype(jnp.float32)).astype(jnp.bfloat16)


def each_place(place, options, body):
    low, high = options[0], options[-1]
    for r in options:
        if low == high:
            body(r)
        elif r == low:
            pl.when(place <= r)(functools.partial(body, r))
        elif r == high:
            pl.when(place >= r)(functools.partial(body, r))
        else:
            pl.when(place == r)(functools.partial(body, r))


def outgoing_kernel(options, has_recv, first, place_ref, *refs):
    out = refs[-1]
    half = out.shape[1]
    rows = pl.ds(first, half)
    owns, others = refs[:len(options)], refs[len(options):2 * len(options)]

    def body(r):
        i = options.index(r)
        for j, piece in enumerate((owns[i], others[i])):
            value = piece[rows, :]
            out[j] = add(value, refs[2 * len(options)][j]) if has_recv else value

    each_place(place_ref[0], options, body)


def incoming_kernel(size, mine, place_ref, *refs):
    out = refs[-1]
    half = out.shape[0] // 2
    count = size - 1

    def body(p):
        for j in range(2):
            rows = pl.ds(j * half, half)
            value = refs[j * count + p - 1][0 if mine else 1]
            if mine:
                value = value.astype(jnp.float32) + refs[2 * count][rows, :].astype(jnp.float32)
                value = (value + refs[2 * count + 1][rows, :].astype(jnp.float32)).astype(jnp.bfloat16)
            out[rows, :] = value

    each_place(place_ref[0], list(range(1, size)), body)


class Chain:
    def __init__(self, size, siblings, place, first, half):
        self.size, self.place, self.first, self.half = size, place, first, half
        self.recv = []
        self.pairs = []
        for z in range(size):
            for m in range(siblings):
                to = z + 1 if m % 2 == 0 else z - 1
                if 0 <= to < size:
                    self.pairs.append((z * siblings + m, to * siblings + m))

    def outgoing(self, t, own, other, after):
        options = [r for r in range(self.size - 1) if 0 <= t - r < len(other)]
        recv = [self.recv[t - 1]] if t > 0 else []
        shape = (2, self.half, own[0].shape[1])
        args = [own[t - r] for r in options] + [other[t - r] for r in options] + recv
        return call(
            functools.partial(outgoing_kernel, options, bool(recv), self.first),
            "outgoing",
            jax.ShapeDtypeStruct(shape, jnp.bfloat16),
            [SMEM] + [VMEM] * len(args) + [ANY] * len(after),
            (self.place, *args, *after),
            bytes_accessed=6 * math.prod(shape),
        )

    def send(self, value):
        self.recv.append(lax.ppermute(value, ("sample", "landmark"), self.pairs))


def incoming(upper, lower, i, own=None, other=None):
    size = upper.size
    args = [chain.recv[i + p - 1] for chain in (upper, lower) for p in range(1, size)]
    mine = own is not None
    if mine:
        args += [own, other]
    shape = (2 * upper.half, args[0].shape[2])
    return call(
        functools.partial(incoming_kernel, size, mine),
        "total" if mine else "incoming",
        jax.ShapeDtypeStruct(shape, jnp.bfloat16),
        [SMEM] + [VMEM] * len(args),
        (upper.place, *args),
        bytes_accessed=8 * math.prod(shape),
    )


def make_local(mesh):
    n_sample = mesh.shape["sample"]
    n_landmark = mesh.shape["landmark"]
    n_all = n_sample * n_landmark
    bits = n_landmark.bit_length() - 1
    siblings = [(m, m ^ 1) for m in range(n_landmark)]

    def order_of(core):
        rest = list(range(1, bits))
        return [0] + (rest if core == 0 else rest[::-1])

    def place_of(core, q):
        return sum(((q >> t) & 1) << bit for t, bit in enumerate(order_of(core)))

    def local(embeddings, landmarks, factor, flips, labels, counts):
        here = lax.axis_index("sample").astype(jnp.int32)
        spot = lax.axis_index("landmark").astype(jnp.int32)
        core = spot % 2
        place = jnp.where(core == 0, here, n_sample - 1 - here).reshape(1)
        here_ref = here.reshape(1)

        pair = own_counts(here_ref, counts, labels, n_sample)
        pair = lax.all_to_all(pair, "sample", 0, 0, tiled=True)
        held, z, scale, signs, mask_a, mask_b = prepare_rows(here_ref, counts, embeddings, landmarks, flips, labels)

        perms = flips.shape[0]
        half = perms // 2
        points = landmarks.shape[0]
        count = points // TILE
        upper = Chain(n_sample, n_landmark, place, 0, half)
        lower = Chain(n_sample, n_landmark, place, half, half)
        own, other, totals = [], [], []
        steps = count + n_sample - 2
        value = None
        for t in range(steps + 1):
            if t < count:
                following = (t + 1) * TILE if t + 1 < count else None
                after = [value] if t > 0 else []
                outs = moments_part(pair, held, z, scale, signs, mask_a, mask_b, landmarks, following, after)
                own.append(outs[0])
                if following is not None:
                    z = outs[1]
            if t > 0:
                after = [own[t]] if t < count else [value]
                lower.send(lower.outgoing(t - 1, own, other, after))
            if t < count:
                other.append(lax.ppermute(own[t], "landmark", siblings))
            if t < steps:
                value = upper.outgoing(t, own, other, totals[-1:])
                upper.send(value)
            i = t - (n_sample - 1)
            if i >= 0:
                share = lax.ppermute(incoming(upper, lower, i), "landmark", siblings)
                totals.append(incoming(upper, lower, i, own[i], share))

        kept_places = [2 * q for q in range(n_landmark // 2)]
        kept_order = sorted(kept_places, key=lambda q: [-((q >> t) & 1) for t in range(1, bits)])
        sent_order = [q + 1 for q in kept_order]

        def table_of(places, order_core):
            zero = jnp.array([place_of(0, q) for q in places], jnp.int32)
            one = jnp.array([place_of(1, q) for q in places], jnp.int32)
            return jnp.bitwise_xor(jnp.where(order_core == 0, zero, one), spot)

        def pairs_of(t):
            return [(m, m ^ (1 << order_of(m % 2)[t])) for m in range(n_landmark)]

        middle = len(kept_order) // 2
        sums = []
        for part in (slice(0, middle), slice(middle, None)):
            sent = whiten(table_of(sent_order[part], 1 - core), factor, totals, n_landmark)
            recv = lax.ppermute(sent, "landmark", siblings)
            kept = whiten(table_of(kept_order[part], core), factor, totals, n_landmark)
            sums.append((kept, recv))
        recv = lax.ppermute(add(*sums[0]), "landmark", pairs_of(1))
        kept = add(*sums[1])
        for t in range(2, bits):
            middle = kept.shape[0] // 2
            sent = add(kept[:middle], recv[:middle])
            kept = add(kept[middle:], recv[middle:])
            recv = lax.ppermute(sent, "landmark", pairs_of(t))
        whitened, share = finish(kept[0], recv[0], n_all)
        share = lax.all_to_all(share, ("sample", "landmark"), 0, 0, tiled=True)
        statistic = jnp.sum(share, axis=0).reshape(perms)
        return whitened, statistic / (points * n_landmark)

    return local


def solution(mesh):
    return jax.shard_map(
        make_local(mesh),
        mesh=mesh,
        in_specs=(
            P("sample", None),
            P("landmark", None),
            P("landmark", "sample"),
            P(None, "sample"),
            P("sample"),
            P(),
        ),
        out_specs=(P(("sample", "landmark"), None), P()),
        check_vma=False,
    )
```

```python
import functools
import math

import jax
import jax.numpy as jnp
from jax import lax
from jax.experimental import pallas as pl
from jax.experimental.pallas import tpu as pltpu
from jax.sharding import PartitionSpec as P

VMEM_LIMIT = 14 * 1024 * 1024
TILE = 256
NT = (((1,), (1,)), ((), ()))


VMEM = pl.BlockSpec(memory_space=pltpu.VMEM)
SMEM = pl.BlockSpec(memory_space=pltpu.SMEM)
HBM = pl.BlockSpec(memory_space=pltpu.HBM)
ANY = pl.BlockSpec(memory_space=pl.ANY)


def in_hbm(x):
    return pltpu.with_memory_space_constraint(x, pltpu.HBM)


def call(kernel, name, out_shape, in_specs, args, flops=0, bytes_accessed=0, transcendentals=0, scratch=()):
    return pl.pallas_call(
        kernel,
        out_shape=out_shape,
        in_specs=in_specs,
        out_specs=jax.tree.map(lambda _: VMEM, out_shape),
        scratch_shapes=list(scratch),
        compiler_params=pltpu.CompilerParams(vmem_limit_bytes=VMEM_LIMIT),
        cost_estimate=pl.CostEstimate(
            flops=flops, bytes_accessed=bytes_accessed, transcendentals=transcendentals
        ),
        name=name,
    )(*args)


def slot_masks(labels, own_count, slots):
    live = slots < own_count
    return (live & (labels == 0)).astype(jnp.float32), (live & (labels != 0)).astype(jnp.float32)


def counts_kernel(here_ref, counts_ref, labels_ref, *refs):
    out_ref = refs[-1]
    own_count = counts_ref[here_ref[0]]
    shape = labels_ref.shape
    slots = lax.broadcasted_iota(jnp.int32, shape, 0) * shape[1] + lax.broadcasted_iota(jnp.int32, shape, 1)
    mask_a, mask_b = slot_masks(labels_ref[...], own_count, slots)
    first = lax.broadcasted_iota(jnp.int32, out_ref.shape[1:], 0) == 0
    pair = jnp.where(first, jnp.sum(mask_a), jnp.sum(mask_b))
    out_ref[...] = jnp.broadcast_to(pair[None], out_ref.shape)


def own_counts(here, counts, labels, copies, after):
    return call(
        counts_kernel,
        "own_counts",
        jax.ShapeDtypeStruct((copies, 8, 128), jnp.float32),
        [SMEM, SMEM, VMEM] + [ANY] * len(after),
        (here, counts, labels.reshape(-1, 128), *after),
    )


def rows_kernel(parts, here_ref, counts_ref, pair_ref, x_ref, z_ref, flips_ref, labels_ref,
                held_ref, first_ref, scale_ref, signs_ref, weight_ref, flips_buf, x_sem, z_sem, f_sem):
    rows, width = x_ref.shape
    block = rows // parts

    def x_copy(i):
        here = pl.ds(i * block, block)
        return pltpu.make_async_copy(x_ref.at[here, :], held_ref.at[here, :], x_sem.at[i])

    flips_copy = pltpu.make_async_copy(flips_ref, flips_buf, f_sem)
    z_copy = pltpu.make_async_copy(z_ref.at[pl.ds(0, first_ref.shape[0]), :], first_ref, z_sem)
    for i in range(parts):
        x_copy(i).start()
    z_copy.start()
    flips_copy.start()
    own_count = counts_ref[here_ref[0]]
    pair = jnp.sum(pair_ref[...], axis=0)
    count_a, count_b = pair[0:1, 0:1], pair[1:2, 0:1]
    balance = jnp.sqrt(count_a * count_b / (count_a + count_b))
    weight_a, weight_b = balance / count_a, balance / count_b
    for j in range(rows // 128):
        here = pl.ds(j * 128, 128)
        labels = jnp.transpose(jnp.broadcast_to(labels_ref[pl.ds(j, 1), :], (128, 128)))[:, 0:1]
        slots = j * 128 + lax.broadcasted_iota(jnp.int32, (128, 1), 0)
        mask_a, mask_b = slot_masks(labels, own_count, slots)
        weight_ref[here, :] = mask_a * weight_a - mask_b * weight_b
    for i in range(parts):
        x_copy(i).wait()
        here = pl.ds(i * block, block)
        x = held_ref[here, :].astype(jnp.float32)
        mean = jnp.sum(x * x, axis=1, keepdims=True) * (1.0 / width)
        scale_ref[here, :] = lax.rsqrt(mean + 1e-06) * (0.5 / math.sqrt(width))
    flips_copy.wait()
    signs_ref[...] = (2 * flips_buf[...] - 1).astype(jnp.bfloat16)
    z_copy.wait()


def prepare_rows(here, counts, pair, x, z, flips, labels):
    rows, width = x.shape
    perms = flips.shape[0]
    parts = 8
    column = jax.ShapeDtypeStruct((rows, 1), jnp.float32)
    return call(
        functools.partial(rows_kernel, parts),
        "prepare_rows",
        [
            pltpu.VMEM((rows, width), x.dtype),
            jax.ShapeDtypeStruct((TILE, width), z.dtype),
            column,
            jax.ShapeDtypeStruct((perms, rows), jnp.bfloat16),
            column,
        ],
        [SMEM, SMEM, VMEM, HBM, HBM, HBM, VMEM],
        (here, counts, pair, in_hbm(x), in_hbm(z), in_hbm(flips), labels.reshape(-1, 128)),
        flops=3 * rows * width,
        bytes_accessed=(rows + TILE) * width * 2 + perms * rows * 4,
        scratch=[
            pltpu.VMEM(flips.shape, flips.dtype),
            pltpu.SemaphoreType.DMA((parts,)),
            pltpu.SemaphoreType.DMA,
            pltpu.SemaphoreType.DMA,
        ],
    )


def moments_kernel(after, next_at_ref, x_ref, z_ref, scale_ref, signs_ref, weight_ref, z_all_ref, *rest):
    out_ref, next_ref, sem = rest[after:]
    at = pl.multiple_of(next_at_ref[0], TILE)
    next_copy = pltpu.make_async_copy(z_all_ref.at[pl.ds(at, TILE), :], next_ref, sem)
    next_copy.start()
    z = z_ref[...]
    z32 = z.astype(jnp.float32)
    mean = jnp.sum(z32 * z32, axis=1, keepdims=True) * (1.0 / z.shape[1])
    point = jnp.broadcast_to(lax.rsqrt(mean + 1e-06), (TILE, 128))
    point_row = jnp.transpose(point)[0:1, :]
    cross = lax.dot_general(x_ref[...], z, NT, preferred_element_type=jnp.float32)
    kern = jnp.exp(cross * scale_ref[...] * point_row)
    weighted = (weight_ref[...] * kern).astype(jnp.bfloat16)
    out_ref[...] = jnp.dot(signs_ref[...], weighted, preferred_element_type=jnp.float32).astype(jnp.bfloat16)
    next_copy.wait()


def moments_part(next_at, x, z, scale, signs, weight, z_all, after):
    rows, width = x.shape
    perms = signs.shape[0]
    return call(
        functools.partial(moments_kernel, len(after)),
        "moments",
        [
            jax.ShapeDtypeStruct((perms, TILE), jnp.bfloat16),
            jax.ShapeDtypeStruct((TILE, width), z.dtype),
        ],
        [SMEM] + [VMEM] * 5 + [HBM] + [ANY] * len(after),
        (next_at, x, z, scale, signs, weight, in_hbm(z_all), *after),
        flops=2 * rows * width * TILE + 2 * perms * rows * TILE,
        bytes_accessed=TILE * width * 2,
        transcendentals=rows * TILE,
        scratch=[pltpu.SemaphoreType.DMA],
    )


def whiten_kernel(table_ref, factor_ref, *refs):
    parts, (out, moments) = refs[:-2], refs[-2:]
    piece = parts[0].shape[1]

    @pl.when(pl.program_id(0) == 0)
    def _():
        for i, part in enumerate(parts):
            moments[:, pl.ds(i * piece, piece)] = part[...]

    out[0] = jnp.dot(moments[...], factor_ref[...], preferred_element_type=jnp.float32).astype(jnp.bfloat16)


def whiten(table, factor, parts, blocks):
    depth, columns = factor.shape
    perms = parts[0].shape[0]
    count = table.shape[0]
    wide = columns // blocks
    return pl.pallas_call(
        whiten_kernel,
        grid_spec=pltpu.PrefetchScalarGridSpec(
            num_scalar_prefetch=1,
            grid=(count,),
            in_specs=[pl.BlockSpec((depth, wide), lambda i, t: (0, t[i]))] + [VMEM] * len(parts),
            out_specs=pl.BlockSpec((1, perms, wide), lambda i, t: (i, 0, 0)),
            scratch_shapes=[pltpu.VMEM((perms, depth), jnp.bfloat16)],
        ),
        out_shape=jax.ShapeDtypeStruct((count, perms, wide), jnp.bfloat16),
        compiler_params=pltpu.CompilerParams(vmem_limit_bytes=VMEM_LIMIT),
        cost_estimate=pl.CostEstimate(
            flops=2 * perms * depth * wide * count,
            bytes_accessed=depth * wide * count * 2,
            transcendentals=0,
        ),
        name="whiten",
    )(table, in_hbm(factor), *parts)


def add_kernel(a_ref, b_ref, *outs):
    at = 0
    for out in outs:
        here = pl.ds(at, out.shape[0])
        out[...] = add(a_ref[here], b_ref[here])
        at += out.shape[0]


def add_blocks(a, b, counts):
    outs = [jax.ShapeDtypeStruct((count,) + a.shape[1:], a.dtype) for count in counts]
    return call(add_kernel, "add_blocks", outs, [VMEM, VMEM], (a, b), bytes_accessed=6 * a.size)


def finish_kernel(a_ref, b_ref, out_ref, share_ref):
    wide = jnp.transpose(a_ref[...].astype(jnp.float32) + b_ref[...].astype(jnp.float32))
    out_ref[...] = wide.astype(jnp.bfloat16)
    share = jnp.sum(wide * wide, axis=0, keepdims=True)
    for j in range(share_ref.shape[1]):
        row = share[:, j * 128:(j + 1) * 128]
        share_ref[:, j, :] = jnp.broadcast_to(row, (share_ref.shape[0], 128))


def finish(a, b, copies):
    perms, wide = a.shape
    return call(
        finish_kernel,
        "finish",
        [
            jax.ShapeDtypeStruct((wide, perms), jnp.bfloat16),
            jax.ShapeDtypeStruct((copies, perms // 128, 128), jnp.float32),
        ],
        [VMEM, VMEM],
        (a, b),
        flops=4 * perms * wide,
        bytes_accessed=perms * wide * 6,
    )


def add(a, b):
    return (a.astype(jnp.float32) + b.astype(jnp.float32)).astype(jnp.bfloat16)


def each_place(place, options, body):
    low, high = options[0], options[-1]
    for r in options:
        if low == high:
            body(r)
        elif r == low:
            pl.when(place <= r)(functools.partial(body, r))
        elif r == high:
            pl.when(place >= r)(functools.partial(body, r))
        else:
            pl.when(place == r)(functools.partial(body, r))


def sum_kernel(terms, depth_ref, *refs):
    out = refs[-1]

    def body(d):
        first, *rest = terms[d]
        if not rest:
            out[...] = refs[first][...]
            return
        value = refs[first][...].astype(jnp.float32)
        for i in rest:
            value = value + refs[i][...].astype(jnp.float32)
        out[...] = value.astype(out.dtype)

    each_place(depth_ref[0], sorted(terms), body)


def sum_at(name, depth, options, after=()):
    args = []
    for arrays in options.values():
        args += [a for a in arrays if not any(a is b for b in args)]
    place = lambda a: next(i for i, b in enumerate(args) if a is b)
    terms = {d: [place(a) for a in arrays] for d, arrays in options.items()}
    return call(
        functools.partial(sum_kernel, terms),
        name,
        jax.ShapeDtypeStruct(args[0].shape, args[0].dtype),
        [SMEM] + [VMEM] * len(args) + [ANY] * len(after),
        (depth, *args, *after),
        bytes_accessed=8 * args[0].size,
    )


class SampleSum:
    def __init__(self, n, depth):
        self.n, self.depth, self.last = n, depth, n // 2 - 1
        self.pieces, self.sent, self.recv = [], {}, {}

    def has(self, c):
        return 0 <= c < len(self.pieces)

    def inner(self, d, c):
        return [self.pieces[c]] + ([self.recv[(d - 1) % 2, c + d - 1]] if d > 0 else [])

    def whole(self, d, c):
        if d == self.last:
            key = (d % 2, c + d)
            return [self.sent[key], self.recv[key]]
        return [self.recv[d % 2, c + self.n - 2 - d]]

    def exchange(self, parity, period, after=()):
        options = {}
        for d in range(self.last + 1):
            if d % 2 == parity:
                if self.has(period - d):
                    options[d] = self.inner(d, period - d)
            elif d > 0 and self.has(period - (self.n - 1 - d)):
                options[d] = self.whole(d, period - (self.n - 1 - d))
        if not options:
            return None
        value = sum_at("exchanged", self.depth, options, after)
        pairs = []
        for i in range(parity, self.n - 1, 2):
            pairs += [(i, i + 1), (i + 1, i)]
        self.sent[parity, period] = value
        self.recv[parity, period] = lax.ppermute(value, "sample", pairs)
        return value

    def total(self, c):
        return sum_at("total", self.depth, {d: self.whole(d, c) for d in range(self.last + 1)})


def make_local(mesh):
    n_sample = mesh.shape["sample"]
    n_landmark = mesh.shape["landmark"]
    n_all = n_sample * n_landmark
    bits = n_landmark.bit_length() - 1
    siblings = [(m, m ^ 1) for m in range(n_landmark)]

    def order_of(core):
        rest = list(range(1, bits))
        return [0] + (rest if core == 0 else rest[::-1])

    def place_of(core, q):
        return sum(((q >> t) & 1) << bit for t, bit in enumerate(order_of(core)))

    def local(embeddings, landmarks, factor, flips, labels, counts):
        here = lax.axis_index("sample").astype(jnp.int32)
        spot = lax.axis_index("landmark").astype(jnp.int32)
        core = spot % 2
        depth = jnp.minimum(here, n_sample - 1 - here).reshape(1)
        here = here.reshape(1)
        points = landmarks.shape[0]
        perms = flips.shape[0]
        count = points // TILE

        kept_places = [2 * q for q in range(n_landmark // 2)]
        kept_order = sorted(kept_places, key=lambda q: [-((q >> t) & 1) for t in range(1, bits)])
        sent_order = [q + 1 for q in kept_order]

        def table_of(places, order_core):
            zero = jnp.array([place_of(0, q) for q in places], jnp.int32)
            one = jnp.array([place_of(1, q) for q in places], jnp.int32)
            return jnp.bitwise_xor(jnp.where(order_core == 0, zero, one), spot)

        def pairs_of(t):
            return [(m, m ^ (1 << order_of(m % 2)[t])) for m in range(n_landmark)]

        middle = len(kept_order) // 2
        tables = [
            (table_of(sent_order[part], 1 - core), table_of(kept_order[part], core))
            for part in (slice(0, middle), slice(middle, None))
        ]
        starts = [jnp.full((1,), (t + 1) % count * TILE, jnp.int32) for t in range(count)]
        after = [depth, *starts, *tables[0], *tables[1]]
        depth, *starts, first_sent, first_kept, second_sent, second_kept = lax.optimization_barrier(after)

        pair = own_counts(here, counts, labels, n_sample, [depth, first_sent, first_kept, second_sent, second_kept])
        pair = lax.all_to_all(pair, "sample", 0, 0, tiled=True)
        held, z, scale, signs, weight = prepare_rows(here, counts, pair, embeddings, landmarks, flips, labels)

        line = SampleSum(n_sample, depth)
        totals = []
        value = None
        for t in range(count + n_sample - 2):
            if t < count:
                after = [value] if t > 0 else []
                piece, z = moments_part(starts[t], held, z, scale, signs, weight, landmarks, after)
                line.pieces.append(piece)
            after = totals[-1:] + line.pieces[-1:]
            value = line.exchange(0, t, after)
            odd = line.exchange(1, t, after)
            value = value if odd is None else odd
            if t >= n_sample - 1:
                totals.append(line.total(t - (n_sample - 1)))
        totals.append(line.total(count - 1))

        sums = []
        for sent_table, kept_table in ((first_sent, first_kept), (second_sent, second_kept)):
            sent = whiten(sent_table, factor, totals, n_landmark)
            recv = lax.ppermute(sent, "landmark", siblings)
            kept = whiten(kept_table, factor, totals, n_landmark)
            (total,) = add_blocks(kept, recv, [kept.shape[0]])
            sums.append(total)
        recv = lax.ppermute(sums[0], "landmark", pairs_of(1))
        kept = sums[1]
        for t in range(2, bits):
            half = kept.shape[0] // 2
            sent, kept = add_blocks(kept, recv, [half, half])
            recv = lax.ppermute(sent, "landmark", pairs_of(t))
        whitened, share = finish(kept[0], recv[0], n_all)
        share = lax.all_to_all(share, ("sample", "landmark"), 0, 0, tiled=True)
        statistic = jnp.sum(share, axis=0).reshape(perms)
        return whitened, statistic / (points * n_landmark)

    return local


def solution(mesh):
    return jax.shard_map(
        make_local(mesh),
        mesh=mesh,
        in_specs=(
            P("sample", None),
            P("landmark", None),
            P("landmark", "sample"),
            P(None, "sample"),
            P("sample"),
            P(),
        ),
        out_specs=(P(("sample", "landmark"), None), P()),
        check_vma=False,
    )
```

```python
import functools
import math

import jax
import jax.numpy as jnp
from jax import lax
from jax.experimental import pallas as pl
from jax.experimental.pallas import tpu as pltpu
from jax.sharding import PartitionSpec as P

VMEM_LIMIT = 10 * 1024 * 1024
TILE = 256
NT = (((1,), (1,)), ((), ()))


VMEM = pl.BlockSpec(memory_space=pltpu.VMEM)
SMEM = pl.BlockSpec(memory_space=pltpu.SMEM)
HBM = pl.BlockSpec(memory_space=pltpu.HBM)
ANY = pl.BlockSpec(memory_space=pl.ANY)


def in_hbm(x):
    return pltpu.with_memory_space_constraint(x, pltpu.HBM)


def call(kernel, name, out_shape, in_specs, args, flops=0, bytes_accessed=0, transcendentals=0, scratch=()):
    return pl.pallas_call(
        kernel,
        out_shape=out_shape,
        in_specs=in_specs,
        out_specs=jax.tree.map(lambda _: VMEM, out_shape),
        scratch_shapes=list(scratch),
        compiler_params=pltpu.CompilerParams(vmem_limit_bytes=VMEM_LIMIT),
        cost_estimate=pl.CostEstimate(
            flops=flops, bytes_accessed=bytes_accessed, transcendentals=transcendentals
        ),
        name=name,
    )(*args)


def slot_masks(labels, own_count, slots):
    live = slots < own_count
    return (live & (labels == 0)).astype(jnp.float32), (live & (labels != 0)).astype(jnp.float32)


def counts_kernel(here_ref, counts_ref, labels_ref, *refs):
    out_ref = refs[-1]
    own_count = counts_ref[here_ref[0]]
    shape = labels_ref.shape
    slots = lax.broadcasted_iota(jnp.int32, shape, 0) * shape[1] + lax.broadcasted_iota(jnp.int32, shape, 1)
    mask_a, mask_b = slot_masks(labels_ref[...], own_count, slots)
    first = lax.broadcasted_iota(jnp.int32, out_ref.shape, 0) == 0
    out_ref[...] = jnp.where(first, jnp.sum(mask_a), jnp.sum(mask_b))


def own_counts(here, counts, labels, after):
    return call(
        counts_kernel,
        "own_counts",
        jax.ShapeDtypeStruct((8, 128), jnp.float32),
        [SMEM, SMEM, VMEM] + [ANY] * len(after),
        (here, counts, labels.reshape(-1, 128), *after),
    )


def weights_kernel(mask_a_ref, mask_b_ref, *refs):
    out = refs[-1]
    pair = refs[0][...]
    for ref in refs[1:-1]:
        pair = pair + ref[...]
    count_a, count_b = pair[0:1, 0:1], pair[1:2, 0:1]
    balance = jnp.sqrt(count_a * count_b / (count_a + count_b))
    out[...] = mask_a_ref[...] * (balance / count_a) - mask_b_ref[...] * (balance / count_b)


def row_weights(mask_a, mask_b, pairs):
    out_shape = jax.ShapeDtypeStruct(mask_a.shape, jnp.float32)
    return call(weights_kernel, "row_weights", out_shape, [VMEM] * (2 + len(pairs)), (mask_a, mask_b, *pairs))


def rows_kernel(parts, here_ref, counts_ref, x_ref, z_ref, flips_ref, labels_ref,
                held_x_ref, held_z_ref, scale_ref, signs_ref, mask_a_ref, mask_b_ref, flips_buf, x_sem, z_sem, f_sem):
    rows, width = x_ref.shape
    block = rows // parts
    tile = z_ref.shape[0] // parts

    def x_copy(i):
        here = pl.ds(i * block, block)
        return pltpu.make_async_copy(x_ref.at[here, :], held_x_ref.at[here, :], x_sem.at[i])

    def z_copy(i):
        here = pl.ds(i * tile, tile)
        return pltpu.make_async_copy(z_ref.at[here, :], held_z_ref.at[here, :], z_sem.at[i])

    flips_copy = pltpu.make_async_copy(flips_ref, flips_buf, f_sem)
    for i in range(parts):
        x_copy(i).start()
    flips_copy.start()
    for i in range(parts):
        z_copy(i).start()
    own_count = counts_ref[here_ref[0]]
    for j in range(rows // 128):
        here = pl.ds(j * 128, 128)
        labels = jnp.transpose(jnp.broadcast_to(labels_ref[pl.ds(j, 1), :], (128, 128)))[:, 0:1]
        slots = j * 128 + lax.broadcasted_iota(jnp.int32, (128, 1), 0)
        mask_a_ref[here, :], mask_b_ref[here, :] = slot_masks(labels, own_count, slots)
    for i in range(parts):
        x_copy(i).wait()
        here = pl.ds(i * block, block)
        x = held_x_ref[here, :].astype(jnp.float32)
        mean = jnp.sum(x * x, axis=1, keepdims=True) * (1.0 / width)
        scale_ref[here, :] = lax.rsqrt(mean + 1e-06) * (0.5 / math.sqrt(width))
    flips_copy.wait()
    signs_ref[...] = (2 * flips_buf[...] - 1).astype(jnp.bfloat16)
    for i in range(parts):
        z_copy(i).wait()


def prepare_rows(here, counts, x, z, flips, labels):
    rows, width = x.shape
    perms = flips.shape[0]
    parts = 8
    column = jax.ShapeDtypeStruct((rows, 1), jnp.float32)
    return call(
        functools.partial(rows_kernel, parts),
        "prepare_rows",
        [
            pltpu.VMEM((rows, width), x.dtype),
            pltpu.VMEM(z.shape, z.dtype),
            column,
            jax.ShapeDtypeStruct((perms, rows), jnp.bfloat16),
            column,
            column,
        ],
        [SMEM, SMEM, HBM, HBM, HBM, VMEM],
        (here, counts, in_hbm(x), in_hbm(z), in_hbm(flips), labels.reshape(-1, 128)),
        flops=3 * rows * width,
        bytes_accessed=(rows + z.shape[0]) * width * 2 + perms * rows * 4,
        scratch=[
            pltpu.VMEM(flips.shape, flips.dtype),
            pltpu.SemaphoreType.DMA((parts,)),
            pltpu.SemaphoreType.DMA((parts,)),
            pltpu.SemaphoreType.DMA,
        ],
    )


def moments_kernel(first, x_ref, z_ref, scale_ref, signs_ref, weight_ref, *rest):
    out_ref = rest[-1]
    z = z_ref[pl.ds(first, TILE), :]
    z32 = z.astype(jnp.float32)
    mean = jnp.sum(z32 * z32, axis=1, keepdims=True) * (1.0 / z.shape[1])
    point = jnp.broadcast_to(lax.rsqrt(mean + 1e-06), (TILE, 128))
    point_row = jnp.transpose(point)[0:1, :]
    cross = lax.dot_general(x_ref[...], z, NT, preferred_element_type=jnp.float32)
    kern = jnp.exp(cross * scale_ref[...] * point_row)
    weighted = (weight_ref[...] * kern).astype(jnp.bfloat16)
    out_ref[...] = jnp.dot(signs_ref[...], weighted, preferred_element_type=jnp.float32).astype(jnp.bfloat16)


def moments_part(first, x, z, scale, signs, weight, after):
    rows, width = x.shape
    perms = signs.shape[0]
    return call(
        functools.partial(moments_kernel, first),
        "moments",
        jax.ShapeDtypeStruct((perms, TILE), jnp.bfloat16),
        [VMEM] * 5 + [ANY] * len(after),
        (x, z, scale, signs, weight, *after),
        flops=2 * rows * width * TILE + 2 * perms * rows * TILE,
        bytes_accessed=TILE * width * 2,
        transcendentals=rows * TILE,
    )


def load_kernel(factor_ref, after_ref, held_ref, sem):
    parts = sem.shape[0]
    block = factor_ref.shape[0] // parts
    copies = []
    for i in range(parts):
        here = pl.ds(i * block, block)
        copies.append(pltpu.make_async_copy(factor_ref.at[here, :], held_ref.at[here, :], sem.at[i]))
        copies[-1].start()
    for copy in copies:
        copy.wait()


def load_factor(factor, after):
    return call(
        load_kernel,
        "load_factor",
        pltpu.VMEM(factor.shape, factor.dtype),
        [HBM, ANY],
        (in_hbm(factor), after),
        bytes_accessed=factor.size * 2,
        scratch=[pltpu.SemaphoreType.DMA((8,))],
    )


def whiten_kernel(table, count, spot_ref, factor_ref, *refs):
    out = refs[-1]
    moments = jnp.concatenate([part[...] for part in refs[:count]], axis=1)
    wide = out.shape[2]
    spot = spot_ref[0]
    for i, (zero, one) in enumerate(table):
        block = jnp.bitwise_xor(jnp.where(spot % 2 == 0, zero, one), spot)
        here = pl.ds(pl.multiple_of(block * wide, wide), wide)
        out[i] = jnp.dot(moments, factor_ref[:, here], preferred_element_type=jnp.float32).astype(jnp.bfloat16)


def whiten(table, spot, factor, parts, blocks, after):
    depth, columns = factor.shape
    perms = parts[0].shape[0]
    count = len(table)
    wide = columns // blocks
    return call(
        functools.partial(whiten_kernel, table, len(parts)),
        "whiten",
        jax.ShapeDtypeStruct((count, perms, wide), jnp.bfloat16),
        [SMEM] + [VMEM] * (1 + len(parts)) + [ANY] * len(after),
        (spot, factor, *parts, *after),
        flops=2 * perms * depth * wide * count,
        bytes_accessed=depth * wide * count * 2,
    )


def add_kernel(a_ref, b_ref, *outs):
    at = 0
    for out in outs:
        here = pl.ds(at, out.shape[0])
        out[...] = add(a_ref[here], b_ref[here])
        at += out.shape[0]


def add_blocks(a, b, counts):
    outs = [jax.ShapeDtypeStruct((count,) + a.shape[1:], a.dtype) for count in counts]
    return call(add_kernel, "add_blocks", outs, [VMEM, VMEM], (a, b), bytes_accessed=6 * a.size)


def finish_kernel(a_ref, b_ref, out_ref, share_ref):
    wide = jnp.transpose(a_ref[...].astype(jnp.float32) + b_ref[...].astype(jnp.float32))
    out_ref[...] = wide.astype(jnp.bfloat16)
    share = jnp.sum(wide * wide, axis=0, keepdims=True)
    for j in range(share_ref.shape[1]):
        row = share[:, j * 128:(j + 1) * 128]
        share_ref[:, j, :] = jnp.broadcast_to(row, (share_ref.shape[0], 128))


def finish(a, b, copies):
    perms, wide = a.shape
    return call(
        finish_kernel,
        "finish",
        [
            jax.ShapeDtypeStruct((wide, perms), jnp.bfloat16),
            jax.ShapeDtypeStruct((copies, perms // 128, 128), jnp.float32),
        ],
        [VMEM, VMEM],
        (a, b),
        flops=4 * perms * wide,
        bytes_accessed=perms * wide * 6,
    )


def add(a, b):
    return (a.astype(jnp.float32) + b.astype(jnp.float32)).astype(jnp.bfloat16)


def each_place(place, options, body):
    low, high = options[0], options[-1]
    for r in options:
        if low == high:
            body(r)
        elif r == low:
            pl.when(place <= r)(functools.partial(body, r))
        elif r == high:
            pl.when(place >= r)(functools.partial(body, r))
        else:
            pl.when(place == r)(functools.partial(body, r))


def sum_kernel(terms, depth_ref, *refs):
    out = refs[-1]

    def body(d):
        first, *rest = terms[d]
        if not rest:
            out[...] = refs[first][...]
            return
        value = refs[first][...].astype(jnp.float32)
        for i in rest:
            value = value + refs[i][...].astype(jnp.float32)
        out[...] = value.astype(out.dtype)

    each_place(depth_ref[0], sorted(terms), body)


def sum_at(name, depth, options, after=()):
    args = []
    for arrays in options.values():
        args += [a for a in arrays if not any(a is b for b in args)]
    place = lambda a: next(i for i, b in enumerate(args) if a is b)
    terms = {d: [place(a) for a in arrays] for d, arrays in options.items()}
    return call(
        functools.partial(sum_kernel, terms),
        name,
        jax.ShapeDtypeStruct(args[0].shape, args[0].dtype),
        [SMEM] + [VMEM] * len(args) + [ANY] * len(after),
        (depth, *args, *after),
        bytes_accessed=8 * args[0].size,
    )


class SampleSum:
    def __init__(self, n, depth):
        self.n, self.depth, self.last = n, depth, n // 2 - 1
        self.pieces, self.sent, self.recv = [], {}, {}

    def has(self, c):
        return 0 <= c < len(self.pieces)

    def inner(self, d, c):
        return [self.pieces[c]] + ([self.recv[(d - 1) % 2, c + d - 1]] if d > 0 else [])

    def whole(self, d, c):
        if d == self.last:
            key = (d % 2, c + d)
            return [self.sent[key], self.recv[key]]
        return [self.recv[d % 2, c + self.n - 2 - d]]

    def exchange(self, parity, period, after=()):
        options = {}
        for d in range(self.last + 1):
            if d % 2 == parity:
                if self.has(period - d):
                    options[d] = self.inner(d, period - d)
            elif d > 0 and self.has(period - (self.n - 1 - d)):
                options[d] = self.whole(d, period - (self.n - 1 - d))
        if not options:
            return None
        value = sum_at("exchanged", self.depth, options, after)
        pairs = []
        for i in range(parity, self.n - 1, 2):
            pairs += [(i, i + 1), (i + 1, i)]
        self.sent[parity, period] = value
        self.recv[parity, period] = lax.ppermute(value, "sample", pairs)
        return value

    def total(self, c):
        return sum_at("total", self.depth, {d: self.whole(d, c) for d in range(self.last + 1)})


def make_local(mesh):
    n_sample = mesh.shape["sample"]
    n_landmark = mesh.shape["landmark"]
    n_all = n_sample * n_landmark
    bits = n_landmark.bit_length() - 1
    siblings = [(m, m ^ 1) for m in range(n_landmark)]

    def order_of(core):
        rest = list(range(1, bits))
        return [0] + (rest if core == 0 else rest[::-1])

    def place_of(core, q):
        return sum(((q >> t) & 1) << bit for t, bit in enumerate(order_of(core)))

    def local(embeddings, landmarks, factor, flips, labels, counts):
        here = lax.axis_index("sample").astype(jnp.int32)
        spot = lax.axis_index("landmark").astype(jnp.int32)
        depth = jnp.minimum(here, n_sample - 1 - here).reshape(1)
        here, spot = here.reshape(1), spot.reshape(1)
        points = landmarks.shape[0]
        perms = flips.shape[0]
        count = points // TILE

        kept_places = [2 * q for q in range(n_landmark // 2)]
        kept_order = sorted(kept_places, key=lambda q: [-((q >> t) & 1) for t in range(1, bits)])
        sent_order = [q + 1 for q in kept_order]

        def table_of(places, swapped):
            cores = (1, 0) if swapped else (0, 1)
            return [tuple(place_of(core, q) for core in cores) for q in places]

        def pairs_of(t):
            return [(m, m ^ (1 << order_of(m % 2)[t])) for m in range(n_landmark)]

        own_pair = own_counts(here, counts, labels, [depth, spot])
        pairs = [own_pair]
        for shift in range(1, n_sample):
            to = [(i, (i + shift) % n_sample) for i in range(n_sample)]
            pairs.append(lax.ppermute(own_pair, "sample", to))
        x, z, scale, signs, mask_a, mask_b = prepare_rows(here, counts, embeddings, landmarks, flips, labels)
        weight = row_weights(mask_a, mask_b, pairs)

        line = SampleSum(n_sample, depth)
        totals = []
        value = None
        for t in range(count + n_sample - 2):
            if t < count:
                after = [value] if t > 0 else []
                line.pieces.append(moments_part(t * TILE, x, z, scale, signs, weight, after))
            after = totals[-1:] + line.pieces[-1:]
            if t == count:
                held_factor = load_factor(factor, value)
                after.append(held_factor)
            for parity in (0, 1) if t < count else (1, 0):
                sent = line.exchange(parity, t, after)
                value = value if sent is None else sent
                if t >= count:
                    after = [value]
            if t >= n_sample - 1:
                totals.append(line.total(t - (n_sample - 1)))
        totals.append(line.total(count - 1))

        middle = len(kept_order) // 2
        sums = []
        for part in (slice(0, middle), slice(middle, None)):
            sent = whiten(table_of(sent_order[part], True), spot, held_factor, totals, n_landmark, sums[-1:])
            recv = lax.ppermute(sent, "landmark", siblings)
            kept = whiten(table_of(kept_order[part], False), spot, held_factor, totals, n_landmark, [sent])
            (total,) = add_blocks(kept, recv, [kept.shape[0]])
            sums.append(total)
        recv = lax.ppermute(sums[0], "landmark", pairs_of(1))
        kept = sums[1]
        for t in range(2, bits):
            half = kept.shape[0] // 2
            sent, kept = add_blocks(kept, recv, [half, half])
            recv = lax.ppermute(sent, "landmark", pairs_of(t))
        whitened, share = finish(kept[0], recv[0], n_all)
        share = lax.all_to_all(share, ("sample", "landmark"), 0, 0, tiled=True)
        statistic = jnp.sum(share, axis=0).reshape(perms)
        return whitened, statistic / (points * n_landmark)

    return local


def solution(mesh):
    return jax.shard_map(
        make_local(mesh),
        mesh=mesh,
        in_specs=(
            P("sample", None),
            P("landmark", None),
            P("landmark", "sample"),
            P(None, "sample"),
            P("sample"),
            P(),
        ),
        out_specs=(P(("sample", "landmark"), None), P()),
        check_vma=False,
    )
```

```python
import functools
import math

import jax
import jax.numpy as jnp
from jax import lax
from jax.experimental import pallas as pl
from jax.experimental.pallas import tpu as pltpu
from jax.sharding import PartitionSpec as P

VMEM_LIMIT = 10 * 1024 * 1024
TILE = 256
NT = (((1,), (1,)), ((), ()))


VMEM = pl.BlockSpec(memory_space=pltpu.VMEM)
SMEM = pl.BlockSpec(memory_space=pltpu.SMEM)
HBM = pl.BlockSpec(memory_space=pltpu.HBM)
ANY = pl.BlockSpec(memory_space=pl.ANY)


def in_hbm(x):
    return pltpu.with_memory_space_constraint(x, pltpu.HBM)


def call(kernel, name, out_shape, in_specs, args, flops=0, bytes_accessed=0, transcendentals=0, scratch=()):
    return pl.pallas_call(
        kernel,
        out_shape=out_shape,
        in_specs=in_specs,
        out_specs=jax.tree.map(lambda _: VMEM, out_shape),
        scratch_shapes=list(scratch),
        compiler_params=pltpu.CompilerParams(vmem_limit_bytes=VMEM_LIMIT),
        cost_estimate=pl.CostEstimate(
            flops=flops, bytes_accessed=bytes_accessed, transcendentals=transcendentals
        ),
        name=name,
    )(*args)


def slot_masks(labels, own_count, slots):
    live = slots < own_count
    return (live & (labels == 0)).astype(jnp.float32), (live & (labels != 0)).astype(jnp.float32)


def counts_kernel(here_ref, counts_ref, labels_ref, *refs):
    out_ref = refs[-1]
    own_count = counts_ref[here_ref[0]]
    shape = labels_ref.shape
    slots = lax.broadcasted_iota(jnp.int32, shape, 0) * shape[1] + lax.broadcasted_iota(jnp.int32, shape, 1)
    mask_a, mask_b = slot_masks(labels_ref[...], own_count, slots)
    first = lax.broadcasted_iota(jnp.int32, out_ref.shape, 0) == 0
    out_ref[...] = jnp.where(first, jnp.sum(mask_a), jnp.sum(mask_b))


def own_counts(here, counts, labels, after):
    return call(
        counts_kernel,
        "own_counts",
        jax.ShapeDtypeStruct((8, 128), jnp.float32),
        [SMEM, SMEM, VMEM] + [ANY] * len(after),
        (here, counts, labels.reshape(-1, 128), *after),
    )


def weights_kernel(mask_a_ref, mask_b_ref, *refs):
    out = refs[-1]
    pair = refs[0][...]
    for ref in refs[1:-1]:
        pair = pair + ref[...]
    count_a, count_b = pair[0:1, 0:1], pair[1:2, 0:1]
    balance = jnp.sqrt(count_a * count_b / (count_a + count_b))
    out[...] = mask_a_ref[...] * (balance / count_a) - mask_b_ref[...] * (balance / count_b)


def row_weights(mask_a, mask_b, pairs):
    out_shape = jax.ShapeDtypeStruct(mask_a.shape, jnp.float32)
    return call(weights_kernel, "row_weights", out_shape, [VMEM] * (2 + len(pairs)), (mask_a, mask_b, *pairs))


def rows_kernel(parts, here_ref, counts_ref, x_ref, z_ref, flips_ref, labels_ref,
                held_x_ref, held_z_ref, scale_ref, signs_ref, mask_a_ref, mask_b_ref, flips_buf, x_sem, z_sem, f_sem):
    rows, width = x_ref.shape
    block = rows // parts
    tile = z_ref.shape[0] // parts

    def x_copy(i):
        here = pl.ds(i * block, block)
        return pltpu.make_async_copy(x_ref.at[here, :], held_x_ref.at[here, :], x_sem.at[i])

    def z_copy(i):
        here = pl.ds(i * tile, tile)
        return pltpu.make_async_copy(z_ref.at[here, :], held_z_ref.at[here, :], z_sem.at[i])

    flips_copy = pltpu.make_async_copy(flips_ref, flips_buf, f_sem)
    for i in range(parts):
        x_copy(i).start()
    flips_copy.start()
    for i in range(parts):
        z_copy(i).start()
    own_count = counts_ref[here_ref[0]]
    for j in range(rows // 128):
        here = pl.ds(j * 128, 128)
        labels = jnp.transpose(jnp.broadcast_to(labels_ref[pl.ds(j, 1), :], (128, 128)))[:, 0:1]
        slots = j * 128 + lax.broadcasted_iota(jnp.int32, (128, 1), 0)
        mask_a_ref[here, :], mask_b_ref[here, :] = slot_masks(labels, own_count, slots)
    for i in range(parts):
        x_copy(i).wait()
        here = pl.ds(i * block, block)
        x = held_x_ref[here, :].astype(jnp.float32)
        mean = jnp.sum(x * x, axis=1, keepdims=True) * (1.0 / width)
        scale_ref[here, :] = lax.rsqrt(mean + 1e-06) * (0.5 / math.sqrt(width))
    flips_copy.wait()
    signs_ref[...] = (2 * flips_buf[...] - 1).astype(jnp.bfloat16)
    for i in range(parts):
        z_copy(i).wait()


def prepare_rows(here, counts, x, z, flips, labels):
    rows, width = x.shape
    perms = flips.shape[0]
    parts = 8
    column = jax.ShapeDtypeStruct((rows, 1), jnp.float32)
    return call(
        functools.partial(rows_kernel, parts),
        "prepare_rows",
        [
            pltpu.VMEM((rows, width), x.dtype),
            pltpu.VMEM(z.shape, z.dtype),
            column,
            jax.ShapeDtypeStruct((perms, rows), jnp.bfloat16),
            column,
            column,
        ],
        [SMEM, SMEM, HBM, HBM, HBM, VMEM],
        (here, counts, in_hbm(x), in_hbm(z), in_hbm(flips), labels.reshape(-1, 128)),
        flops=3 * rows * width,
        bytes_accessed=(rows + z.shape[0]) * width * 2 + perms * rows * 4,
        scratch=[
            pltpu.VMEM(flips.shape, flips.dtype),
            pltpu.SemaphoreType.DMA((parts,)),
            pltpu.SemaphoreType.DMA((parts,)),
            pltpu.SemaphoreType.DMA,
        ],
    )


def moments_kernel(first, x_ref, z_ref, scale_ref, signs_ref, weight_ref, *rest):
    out_ref = rest[-1]
    z = z_ref[pl.ds(first, TILE), :]
    z32 = z.astype(jnp.float32)
    mean = jnp.sum(z32 * z32, axis=1, keepdims=True) * (1.0 / z.shape[1])
    point = jnp.broadcast_to(lax.rsqrt(mean + 1e-06), (TILE, 128))
    point_row = jnp.transpose(point)[0:1, :]
    cross = lax.dot_general(x_ref[...], z, NT, preferred_element_type=jnp.float32)
    kern = jnp.exp(cross * scale_ref[...] * point_row)
    weighted = (weight_ref[...] * kern).astype(jnp.bfloat16)
    out_ref[...] = jnp.dot(signs_ref[...], weighted, preferred_element_type=jnp.float32).astype(jnp.bfloat16)


def moments_part(first, x, z, scale, signs, weight, after):
    rows, width = x.shape
    perms = signs.shape[0]
    return call(
        functools.partial(moments_kernel, first),
        "moments",
        jax.ShapeDtypeStruct((perms, TILE), jnp.bfloat16),
        [VMEM] * 5 + [ANY] * len(after),
        (x, z, scale, signs, weight, *after),
        flops=2 * rows * width * TILE + 2 * perms * rows * TILE,
        bytes_accessed=TILE * width * 2,
        transcendentals=rows * TILE,
    )


def load_kernel(factor_ref, *refs):
    held_ref, sem = refs[-2:]
    parts = sem.shape[0]
    block = factor_ref.shape[0] // parts
    copies = []
    for i in range(parts):
        here = pl.ds(i * block, block)
        copies.append(pltpu.make_async_copy(factor_ref.at[here, :], held_ref.at[here, :], sem.at[i]))
        copies[-1].start()
    for copy in copies:
        copy.wait()


def load_factor(factor, after):
    return call(
        load_kernel,
        "load_factor",
        pltpu.VMEM(factor.shape, factor.dtype),
        [HBM] + [ANY] * len(after),
        (in_hbm(factor), *after),
        bytes_accessed=factor.size * 2,
        scratch=[pltpu.SemaphoreType.DMA((8,))],
    )


def whiten_kernel(table, count, spot_ref, factor_ref, *refs):
    out = refs[-1]
    moments = jnp.concatenate([part[...] for part in refs[:count]], axis=1)
    wide = out.shape[2]
    spot = spot_ref[0]
    for i, (zero, one) in enumerate(table):
        block = jnp.bitwise_xor(jnp.where(spot % 2 == 0, zero, one), spot)
        here = pl.ds(pl.multiple_of(block * wide, wide), wide)
        out[i] = jnp.dot(moments, factor_ref[:, here], preferred_element_type=jnp.float32).astype(jnp.bfloat16)


def whiten(table, spot, factor, parts, blocks, after):
    depth, columns = factor.shape
    perms = parts[0].shape[0]
    count = len(table)
    wide = columns // blocks
    return call(
        functools.partial(whiten_kernel, table, len(parts)),
        "whiten",
        jax.ShapeDtypeStruct((count, perms, wide), jnp.bfloat16),
        [SMEM] + [VMEM] * (1 + len(parts)) + [ANY] * len(after),
        (spot, factor, *parts, *after),
        flops=2 * perms * depth * wide * count,
        bytes_accessed=depth * wide * count * 2,
    )


def add_kernel(a_ref, b_ref, *outs):
    at = 0
    for out in outs:
        here = pl.ds(at, out.shape[0])
        out[...] = add(a_ref[here], b_ref[here])
        at += out.shape[0]


def add_blocks(a, b, counts):
    outs = [jax.ShapeDtypeStruct((count,) + a.shape[1:], a.dtype) for count in counts]
    return call(add_kernel, "add_blocks", outs, [VMEM, VMEM], (a, b), bytes_accessed=6 * a.size)


def finish_kernel(a_ref, b_ref, out_ref, share_ref):
    wide = jnp.transpose(a_ref[...].astype(jnp.float32) + b_ref[...].astype(jnp.float32))
    out_ref[...] = wide.astype(jnp.bfloat16)
    share = jnp.sum(wide * wide, axis=0, keepdims=True)
    for j in range(share_ref.shape[1]):
        row = share[:, j * 128:(j + 1) * 128]
        share_ref[:, j, :] = jnp.broadcast_to(row, (share_ref.shape[0], 128))


def finish(a, b, copies):
    perms, wide = a.shape
    return call(
        finish_kernel,
        "finish",
        [
            jax.ShapeDtypeStruct((wide, perms), jnp.bfloat16),
            jax.ShapeDtypeStruct((copies, perms // 128, 128), jnp.float32),
        ],
        [VMEM, VMEM],
        (a, b),
        flops=4 * perms * wide,
        bytes_accessed=perms * wide * 6,
    )


def add(a, b):
    return (a.astype(jnp.float32) + b.astype(jnp.float32)).astype(jnp.bfloat16)


def each_place(place, options, body):
    low, high = options[0], options[-1]
    for r in options:
        if low == high:
            body(r)
        elif r == low:
            pl.when(place <= r)(functools.partial(body, r))
        elif r == high:
            pl.when(place >= r)(functools.partial(body, r))
        else:
            pl.when(place == r)(functools.partial(body, r))


def sum_kernel(terms, depth_ref, *refs):
    out = refs[-1]

    def body(d):
        first, *rest = terms[d]
        if not rest:
            out[...] = refs[first][...]
            return
        value = refs[first][...].astype(jnp.float32)
        for i in rest:
            value = value + refs[i][...].astype(jnp.float32)
        out[...] = value.astype(out.dtype)

    each_place(depth_ref[0], sorted(terms), body)


def sum_at(name, depth, options, after=()):
    args = []
    for arrays in options.values():
        args += [a for a in arrays if not any(a is b for b in args)]
    place = lambda a: next(i for i, b in enumerate(args) if a is b)
    terms = {d: [place(a) for a in arrays] for d, arrays in options.items()}
    return call(
        functools.partial(sum_kernel, terms),
        name,
        jax.ShapeDtypeStruct(args[0].shape, args[0].dtype),
        [SMEM] + [VMEM] * len(args) + [ANY] * len(after),
        (depth, *args, *after),
        bytes_accessed=8 * args[0].size,
    )


class SampleSum:
    def __init__(self, n, depth):
        self.n, self.depth, self.last = n, depth, n // 2 - 1
        self.pieces, self.sent, self.recv = [], {}, {}

    def has(self, c):
        return 0 <= c < len(self.pieces)

    def inner(self, d, c):
        return [self.pieces[c]] + ([self.recv[(d - 1) % 2, c + d - 1]] if d > 0 else [])

    def whole(self, d, c):
        if d == self.last:
            key = (d % 2, c + d)
            return [self.sent[key], self.recv[key]]
        return [self.recv[d % 2, c + self.n - 1 - d]]

    def exchange(self, parity, period, after=()):
        options = {}
        for d in range(self.last + 1):
            if d % 2 == parity:
                if self.has(period - d):
                    options[d] = self.inner(d, period - d)
            elif d > 0 and self.has(period - (self.n - d)):
                options[d] = self.whole(d, period - (self.n - d))
        if not options:
            return None
        value = sum_at("exchanged", self.depth, options, after)
        pairs = []
        for i in range(parity, self.n - 1, 2):
            pairs += [(i, i + 1), (i + 1, i)]
        self.sent[parity, period] = value
        self.recv[parity, period] = lax.ppermute(value, "sample", pairs)
        return value

    def total(self, c):
        return sum_at("total", self.depth, {d: self.whole(d, c) for d in range(self.last + 1)})


def make_local(mesh):
    n_sample = mesh.shape["sample"]
    n_landmark = mesh.shape["landmark"]
    n_all = n_sample * n_landmark
    bits = n_landmark.bit_length() - 1
    siblings = [(m, m ^ 1) for m in range(n_landmark)]

    def order_of(core):
        rest = list(range(1, bits))
        return [0] + (rest if core == 0 else rest[::-1])

    def place_of(core, q):
        return sum(((q >> t) & 1) << bit for t, bit in enumerate(order_of(core)))

    def local(embeddings, landmarks, factor, flips, labels, counts):
        here = lax.axis_index("sample").astype(jnp.int32)
        spot = lax.axis_index("landmark").astype(jnp.int32)
        depth = jnp.minimum(here, n_sample - 1 - here).reshape(1)
        here, spot = here.reshape(1), spot.reshape(1)
        points = landmarks.shape[0]
        perms = flips.shape[0]
        count = points // TILE

        kept_places = [2 * q for q in range(n_landmark // 2)]
        kept_order = sorted(kept_places, key=lambda q: [-((q >> t) & 1) for t in range(1, bits)])
        sent_order = [q + 1 for q in kept_order]

        def table_of(places, swapped):
            cores = (1, 0) if swapped else (0, 1)
            return [tuple(place_of(core, q) for core in cores) for q in places]

        def pairs_of(t):
            return [(m, m ^ (1 << order_of(m % 2)[t])) for m in range(n_landmark)]

        own_pair = own_counts(here, counts, labels, [depth, spot])
        pairs = [own_pair]
        for shift in range(1, n_sample):
            to = [(i, (i + shift) % n_sample) for i in range(n_sample)]
            pairs.append(lax.ppermute(own_pair, "sample", to))
        x, z, scale, signs, mask_a, mask_b = prepare_rows(here, counts, embeddings, landmarks, flips, labels)
        weight = row_weights(mask_a, mask_b, pairs)

        line = SampleSum(n_sample, depth)
        totals = []
        value = None
        for t in range(count + n_sample - 1):
            if t < count:
                after = [value] if t > 0 else []
                after += [line.recv[1, t - 2]] if (1, t - 2) in line.recv else []
                line.pieces.append(moments_part(t * TILE, x, z, scale, signs, weight, after))
            after = totals[-1:] + line.pieces[-1:]
            if t == count:
                held_factor = load_factor(factor, [value, line.recv[1, t - 2]])
                after.append(held_factor)
            for parity in (1, 0):
                sent = line.exchange(parity, t, after)
                if sent is not None:
                    value, after = sent, [sent]
            if t >= n_sample:
                totals.append(line.total(t - n_sample))
        totals.append(line.total(count - 1))

        middle = len(kept_order) // 2
        sums = []
        for part in (slice(0, middle), slice(middle, None)):
            sent = whiten(table_of(sent_order[part], True), spot, held_factor, totals, n_landmark, sums[-1:])
            recv = lax.ppermute(sent, "landmark", siblings)
            kept = whiten(table_of(kept_order[part], False), spot, held_factor, totals, n_landmark, [sent])
            (total,) = add_blocks(kept, recv, [kept.shape[0]])
            sums.append(total)
        recv = lax.ppermute(sums[0], "landmark", pairs_of(1))
        kept = sums[1]
        for t in range(2, bits):
            half = kept.shape[0] // 2
            sent, kept = add_blocks(kept, recv, [half, half])
            recv = lax.ppermute(sent, "landmark", pairs_of(t))
        whitened, share = finish(kept[0], recv[0], n_all)
        share = lax.all_to_all(share, ("sample", "landmark"), 0, 0, tiled=True)
        statistic = jnp.sum(share, axis=0).reshape(perms)
        return whitened, statistic / (points * n_landmark)

    return local


def solution(mesh):
    return jax.shard_map(
        make_local(mesh),
        mesh=mesh,
        in_specs=(
            P("sample", None),
            P("landmark", None),
            P("landmark", "sample"),
            P(None, "sample"),
            P("sample"),
            P(),
        ),
        out_specs=(P(("sample", "landmark"), None), P()),
        check_vma=False,
    )
```

```python
import functools
import math

import jax
import jax.numpy as jnp
from jax import lax
from jax.experimental import pallas as pl
from jax.experimental.pallas import tpu as pltpu
from jax.sharding import PartitionSpec as P

VMEM_LIMIT = 10 * 1024 * 1024
TILE = 256
NT = (((1,), (1,)), ((), ()))


VMEM = pl.BlockSpec(memory_space=pltpu.VMEM)
SMEM = pl.BlockSpec(memory_space=pltpu.SMEM)
HBM = pl.BlockSpec(memory_space=pltpu.HBM)
ANY = pl.BlockSpec(memory_space=pl.ANY)


def in_hbm(x):
    return pltpu.with_memory_space_constraint(x, pltpu.HBM)


def call(kernel, name, out_shape, in_specs, args, flops=0, bytes_accessed=0, transcendentals=0, scratch=()):
    return pl.pallas_call(
        kernel,
        out_shape=out_shape,
        in_specs=in_specs,
        out_specs=jax.tree.map(lambda _: VMEM, out_shape),
        scratch_shapes=list(scratch),
        compiler_params=pltpu.CompilerParams(vmem_limit_bytes=VMEM_LIMIT),
        cost_estimate=pl.CostEstimate(
            flops=flops, bytes_accessed=bytes_accessed, transcendentals=transcendentals
        ),
        name=name,
    )(*args)


def slot_masks(labels, own_count, slots):
    live = slots < own_count
    return (live & (labels == 0)).astype(jnp.float32), (live & (labels != 0)).astype(jnp.float32)


def counts_kernel(here_ref, counts_ref, labels_ref, *refs):
    out_ref = refs[-1]
    own_count = counts_ref[here_ref[0]]
    shape = labels_ref.shape
    slots = lax.broadcasted_iota(jnp.int32, shape, 0) * shape[1] + lax.broadcasted_iota(jnp.int32, shape, 1)
    mask_a, mask_b = slot_masks(labels_ref[...], own_count, slots)
    first = lax.broadcasted_iota(jnp.int32, out_ref.shape, 0) == 0
    out_ref[...] = jnp.where(first, jnp.sum(mask_a), jnp.sum(mask_b))


def own_counts(here, counts, labels, after):
    return call(
        counts_kernel,
        "own_counts",
        jax.ShapeDtypeStruct((8, 128), jnp.float32),
        [SMEM, SMEM, VMEM] + [ANY] * len(after),
        (here, counts, labels.reshape(-1, 128), *after),
    )


def weights_kernel(mask_a_ref, mask_b_ref, *refs):
    out = refs[-1]
    pair = refs[0][...]
    for ref in refs[1:-1]:
        pair = pair + ref[...]
    count_a, count_b = pair[0:1, 0:1], pair[1:2, 0:1]
    balance = jnp.sqrt(count_a * count_b / (count_a + count_b))
    out[...] = mask_a_ref[...] * (balance / count_a) - mask_b_ref[...] * (balance / count_b)


def row_weights(mask_a, mask_b, pairs):
    out_shape = jax.ShapeDtypeStruct(mask_a.shape, jnp.float32)
    return call(weights_kernel, "row_weights", out_shape, [VMEM] * (2 + len(pairs)), (mask_a, mask_b, *pairs))


def rows_kernel(parts, here_ref, counts_ref, x_ref, z_ref, flips_ref, labels_ref,
                held_x_ref, held_z_ref, scale_ref, signs_ref, mask_a_ref, mask_b_ref, flips_buf, x_sem, z_sem, f_sem):
    rows, width = x_ref.shape
    block = rows // parts

    def x_copy(i):
        here = pl.ds(i * block, block)
        return pltpu.make_async_copy(x_ref.at[here, :], held_x_ref.at[here, :], x_sem.at[i])

    z_copy = pltpu.make_async_copy(z_ref.at[pl.ds(0, TILE), :], held_z_ref, z_sem)
    flips_copy = pltpu.make_async_copy(flips_ref, flips_buf, f_sem)
    for i in range(parts):
        x_copy(i).start()
    flips_copy.start()
    z_copy.start()
    own_count = counts_ref[here_ref[0]]
    for j in range(rows // 128):
        here = pl.ds(j * 128, 128)
        labels = jnp.transpose(jnp.broadcast_to(labels_ref[pl.ds(j, 1), :], (128, 128)))[:, 0:1]
        slots = j * 128 + lax.broadcasted_iota(jnp.int32, (128, 1), 0)
        mask_a_ref[here, :], mask_b_ref[here, :] = slot_masks(labels, own_count, slots)
    for i in range(parts):
        x_copy(i).wait()
        here = pl.ds(i * block, block)
        x = held_x_ref[here, :].astype(jnp.float32)
        mean = jnp.sum(x * x, axis=1, keepdims=True) * (1.0 / width)
        scale_ref[here, :] = lax.rsqrt(mean + 1e-06) * (0.5 / math.sqrt(width))
    flips_copy.wait()
    signs_ref[...] = (2 * flips_buf[...] - 1).astype(jnp.bfloat16)
    z_copy.wait()


def prepare_rows(here, counts, x, z, flips, labels):
    rows, width = x.shape
    perms = flips.shape[0]
    parts = 8
    column = jax.ShapeDtypeStruct((rows, 1), jnp.float32)
    return call(
        functools.partial(rows_kernel, parts),
        "prepare_rows",
        [
            pltpu.VMEM((rows, width), x.dtype),
            pltpu.VMEM((TILE, width), z.dtype),
            column,
            jax.ShapeDtypeStruct((perms, rows), jnp.bfloat16),
            column,
            column,
        ],
        [SMEM, SMEM, HBM, HBM, HBM, VMEM],
        (here, counts, in_hbm(x), in_hbm(z), in_hbm(flips), labels.reshape(-1, 128)),
        flops=3 * rows * width,
        bytes_accessed=(rows + TILE) * width * 2 + perms * rows * 4,
        scratch=[
            pltpu.VMEM(flips.shape, flips.dtype),
            pltpu.SemaphoreType.DMA((parts,)),
            pltpu.SemaphoreType.DMA,
            pltpu.SemaphoreType.DMA,
        ],
    )


def row_copies(source, at, target, sem):
    parts = sem.shape[0]
    block = target.shape[0] // parts
    copies = []
    for i in range(parts):
        rows = source.at[pl.ds(at + i * block, block), :]
        copies.append(pltpu.make_async_copy(rows, target.at[pl.ds(i * block, block), :], sem.at[i]))
    return copies


def moments_kernel(first, loads, x_ref, z_ref, scale_ref, signs_ref, weight_ref, *rest):
    copies = []
    if loads:
        z_all_ref, out_ref, held_ref, sem = rest
        copies = row_copies(z_all_ref, TILE, held_ref, sem)
    else:
        out_ref = rest[-1]
    for copy in copies:
        copy.start()
    z = z_ref[pl.ds(first, TILE), :]
    z32 = z.astype(jnp.float32)
    mean = jnp.sum(z32 * z32, axis=1, keepdims=True) * (1.0 / z.shape[1])
    point = jnp.broadcast_to(lax.rsqrt(mean + 1e-06), (TILE, 128))
    point_row = jnp.transpose(point)[0:1, :]
    cross = lax.dot_general(x_ref[...], z, NT, preferred_element_type=jnp.float32)
    kern = jnp.exp(cross * scale_ref[...] * point_row)
    weighted = (weight_ref[...] * kern).astype(jnp.bfloat16)
    out_ref[...] = jnp.dot(signs_ref[...], weighted, preferred_element_type=jnp.float32).astype(jnp.bfloat16)
    for copy in copies:
        copy.wait()


def moments_part(first, x, z, scale, signs, weight, after=(), z_all=None):
    rows, width = x.shape
    perms = signs.shape[0]
    out_shape = [jax.ShapeDtypeStruct((perms, TILE), jnp.bfloat16)]
    in_specs, args, scratch = [VMEM] * 5, [x, z, scale, signs, weight], []
    if z_all is not None:
        others = z_all.shape[0] - TILE
        out_shape.append(pltpu.VMEM((others, width), z.dtype))
        in_specs, args = in_specs + [HBM], args + [in_hbm(z_all)]
        scratch = [pltpu.SemaphoreType.DMA((others // TILE,))]
    return call(
        functools.partial(moments_kernel, first, z_all is not None),
        "moments",
        out_shape,
        in_specs + [ANY] * len(after),
        (*args, *after),
        flops=2 * rows * width * TILE + 2 * perms * rows * TILE,
        bytes_accessed=TILE * width * 2,
        transcendentals=rows * TILE,
        scratch=scratch,
    )


def load_kernel(factor_ref, *refs):
    held_ref, sem = refs[-2:]
    copies = row_copies(factor_ref, 0, held_ref, sem)
    for copy in copies:
        copy.start()
    for copy in copies:
        copy.wait()


def load_factor(factor, after):
    return call(
        load_kernel,
        "load_factor",
        pltpu.VMEM(factor.shape, factor.dtype),
        [HBM] + [ANY] * len(after),
        (in_hbm(factor), *after),
        bytes_accessed=factor.size * 2,
        scratch=[pltpu.SemaphoreType.DMA((8,))],
    )


def whiten_kernel(table, count, spot_ref, factor_ref, *refs):
    out = refs[-1]
    moments = jnp.concatenate([part[...] for part in refs[:count]], axis=1)
    wide = out.shape[2]
    spot = spot_ref[0]
    for i, (zero, one) in enumerate(table):
        block = jnp.bitwise_xor(jnp.where(spot % 2 == 0, zero, one), spot)
        here = pl.ds(pl.multiple_of(block * wide, wide), wide)
        out[i] = jnp.dot(moments, factor_ref[:, here], preferred_element_type=jnp.float32).astype(jnp.bfloat16)


def whiten(table, spot, factor, parts, blocks, after):
    depth, columns = factor.shape
    perms = parts[0].shape[0]
    count = len(table)
    wide = columns // blocks
    return call(
        functools.partial(whiten_kernel, table, len(parts)),
        "whiten",
        jax.ShapeDtypeStruct((count, perms, wide), jnp.bfloat16),
        [SMEM] + [VMEM] * (1 + len(parts)) + [ANY] * len(after),
        (spot, factor, *parts, *after),
        flops=2 * perms * depth * wide * count,
        bytes_accessed=depth * wide * count * 2,
    )


def add_kernel(a_ref, b_ref, *outs):
    at = 0
    for out in outs:
        here = pl.ds(at, out.shape[0])
        out[...] = add(a_ref[here], b_ref[here])
        at += out.shape[0]


def add_blocks(a, b, counts):
    outs = [jax.ShapeDtypeStruct((count,) + a.shape[1:], a.dtype) for count in counts]
    return call(add_kernel, "add_blocks", outs, [VMEM, VMEM], (a, b), bytes_accessed=6 * a.size)


def finish_kernel(a_ref, b_ref, out_ref, share_ref):
    wide = jnp.transpose(a_ref[...].astype(jnp.float32) + b_ref[...].astype(jnp.float32))
    out_ref[...] = wide.astype(jnp.bfloat16)
    share = jnp.sum(wide * wide, axis=0, keepdims=True)
    for j in range(share_ref.shape[1]):
        row = share[:, j * 128:(j + 1) * 128]
        share_ref[:, j, :] = jnp.broadcast_to(row, (share_ref.shape[0], 128))


def finish(a, b, copies):
    perms, wide = a.shape
    return call(
        finish_kernel,
        "finish",
        [
            jax.ShapeDtypeStruct((wide, perms), jnp.bfloat16),
            jax.ShapeDtypeStruct((copies, perms // 128, 128), jnp.float32),
        ],
        [VMEM, VMEM],
        (a, b),
        flops=4 * perms * wide,
        bytes_accessed=perms * wide * 6,
    )


def add(a, b):
    return (a.astype(jnp.float32) + b.astype(jnp.float32)).astype(jnp.bfloat16)


def each_place(place, options, body):
    low, high = options[0], options[-1]
    for r in options:
        if low == high:
            body(r)
        elif r == low:
            pl.when(place <= r)(functools.partial(body, r))
        elif r == high:
            pl.when(place >= r)(functools.partial(body, r))
        else:
            pl.when(place == r)(functools.partial(body, r))


def sum_kernel(terms, depth_ref, *refs):
    out = refs[-1]

    def body(d):
        first, *rest = terms[d]
        if not rest:
            out[...] = refs[first][...]
            return
        value = refs[first][...].astype(jnp.float32)
        for i in rest:
            value = value + refs[i][...].astype(jnp.float32)
        out[...] = value.astype(out.dtype)

    each_place(depth_ref[0], sorted(terms), body)


def sum_at(name, depth, options, after=()):
    args = []
    for arrays in options.values():
        args += [a for a in arrays if not any(a is b for b in args)]
    place = lambda a: next(i for i, b in enumerate(args) if a is b)
    terms = {d: [place(a) for a in arrays] for d, arrays in options.items()}
    return call(
        functools.partial(sum_kernel, terms),
        name,
        jax.ShapeDtypeStruct(args[0].shape, args[0].dtype),
        [SMEM] + [VMEM] * len(args) + [ANY] * len(after),
        (depth, *args, *after),
        bytes_accessed=8 * args[0].size,
    )


class SampleSum:
    def __init__(self, n, depth):
        self.n, self.depth, self.last = n, depth, n // 2 - 1
        self.pieces, self.sent, self.recv = [], {}, {}

    def has(self, c):
        return 0 <= c < len(self.pieces)

    def inner(self, d, c):
        return [self.pieces[c]] + ([self.recv[(d - 1) % 2, c + d - 1]] if d > 0 else [])

    def whole(self, d, c):
        if d == self.last:
            key = (d % 2, c + d)
            return [self.sent[key], self.recv[key]]
        return [self.recv[d % 2, c + self.n - 1 - d]]

    def exchange(self, parity, period, after=()):
        options = {}
        for d in range(self.last + 1):
            if d % 2 == parity:
                if self.has(period - d):
                    options[d] = self.inner(d, period - d)
            elif d > 0 and self.has(period - (self.n - d)):
                options[d] = self.whole(d, period - (self.n - d))
        if not options:
            return None
        value = sum_at("exchanged", self.depth, options, after)
        pairs = []
        for i in range(parity, self.n - 1, 2):
            pairs += [(i, i + 1), (i + 1, i)]
        self.sent[parity, period] = value
        self.recv[parity, period] = lax.ppermute(value, "sample", pairs)
        return value

    def total(self, c):
        return sum_at("total", self.depth, {d: self.whole(d, c) for d in range(self.last + 1)})


def make_local(mesh):
    n_sample = mesh.shape["sample"]
    n_landmark = mesh.shape["landmark"]
    n_all = n_sample * n_landmark
    bits = n_landmark.bit_length() - 1
    siblings = [(m, m ^ 1) for m in range(n_landmark)]

    def order_of(core):
        rest = list(range(1, bits))
        return [0] + (rest if core == 0 else rest[::-1])

    def place_of(core, q):
        return sum(((q >> t) & 1) << bit for t, bit in enumerate(order_of(core)))

    def local(embeddings, landmarks, factor, flips, labels, counts):
        here = lax.axis_index("sample").astype(jnp.int32)
        spot = lax.axis_index("landmark").astype(jnp.int32)
        depth = jnp.minimum(here, n_sample - 1 - here).reshape(1)
        here, spot = here.reshape(1), spot.reshape(1)
        points = landmarks.shape[0]
        perms = flips.shape[0]
        count = points // TILE

        kept_places = [2 * q for q in range(n_landmark // 2)]
        kept_order = sorted(kept_places, key=lambda q: [-((q >> t) & 1) for t in range(1, bits)])
        sent_order = [q + 1 for q in kept_order]

        def table_of(places, swapped):
            cores = (1, 0) if swapped else (0, 1)
            return [tuple(place_of(core, q) for core in cores) for q in places]

        def pairs_of(t):
            return [(m, m ^ (1 << order_of(m % 2)[t])) for m in range(n_landmark)]

        own_pair = own_counts(here, counts, labels, [depth, spot])
        pairs = [own_pair]
        for shift in range(1, n_sample):
            to = [(i, (i + shift) % n_sample) for i in range(n_sample)]
            pairs.append(lax.ppermute(own_pair, "sample", to))
        x, z, scale, signs, mask_a, mask_b = prepare_rows(here, counts, embeddings, landmarks, flips, labels)
        weight = row_weights(mask_a, mask_b, pairs)

        line = SampleSum(n_sample, depth)
        totals = []
        value = None
        for t in range(count + n_sample - 1):
            if t == 0:
                piece, z = moments_part(0, x, z, scale, signs, weight, z_all=landmarks)
                line.pieces.append(piece)
            elif t < count:
                after = [value] + ([line.recv[1, t - 2]] if (1, t - 2) in line.recv else [])
                line.pieces += moments_part((t - 1) * TILE, x, z, scale, signs, weight, after)
            after = totals[-1:] + line.pieces[-1:]
            if t == count + n_sample - 2:
                after.append(held_factor)
            if t == count:
                after.append(line.recv[1, t - 2])
            for parity in (1, 0):
                sent = line.exchange(parity, t, after)
                if sent is not None:
                    value, after = sent, [sent]
            if t == count:
                held_factor = load_factor(factor, [value, line.recv[1, t - 1]])
            if t >= n_sample:
                totals.append(line.total(t - n_sample))
        totals.append(line.total(count - 1))

        middle = len(kept_order) // 2
        sums = []
        for part in (slice(0, middle), slice(middle, None)):
            sent = whiten(table_of(sent_order[part], True), spot, held_factor, totals, n_landmark, sums[-1:])
            recv = lax.ppermute(sent, "landmark", siblings)
            kept = whiten(table_of(kept_order[part], False), spot, held_factor, totals, n_landmark, [sent])
            (total,) = add_blocks(kept, recv, [kept.shape[0]])
            sums.append(total)
        recv = lax.ppermute(sums[0], "landmark", pairs_of(1))
        kept = sums[1]
        for t in range(2, bits):
            half = kept.shape[0] // 2
            sent, kept = add_blocks(kept, recv, [half, half])
            recv = lax.ppermute(sent, "landmark", pairs_of(t))
        whitened, share = finish(kept[0], recv[0], n_all)
        share = lax.all_to_all(share, ("sample", "landmark"), 0, 0, tiled=True)
        statistic = jnp.sum(share, axis=0).reshape(perms)
        return whitened, statistic / (points * n_landmark)

    return local


def solution(mesh):
    return jax.shard_map(
        make_local(mesh),
        mesh=mesh,
        in_specs=(
            P("sample", None),
            P("landmark", None),
            P("landmark", "sample"),
            P(None, "sample"),
            P("sample"),
            P(),
        ),
        out_specs=(P(("sample", "landmark"), None), P()),
        check_vma=False,
    )
```

```python
import functools
import math

import jax
import jax.numpy as jnp
from jax import lax
from jax.experimental import pallas as pl
from jax.experimental.pallas import tpu as pltpu
from jax.sharding import PartitionSpec as P

VMEM_LIMIT = 10 * 1024 * 1024
TILE = 256
NT = (((1,), (1,)), ((), ()))


VMEM = pl.BlockSpec(memory_space=pltpu.VMEM)
SMEM = pl.BlockSpec(memory_space=pltpu.SMEM)
HBM = pl.BlockSpec(memory_space=pltpu.HBM)
ANY = pl.BlockSpec(memory_space=pl.ANY)


def in_hbm(x):
    return pltpu.with_memory_space_constraint(x, pltpu.HBM)


def call(kernel, name, out_shape, in_specs, args, flops=0, bytes_accessed=0, transcendentals=0, scratch=()):
    return pl.pallas_call(
        kernel,
        out_shape=out_shape,
        in_specs=in_specs,
        out_specs=jax.tree.map(lambda _: VMEM, out_shape),
        scratch_shapes=list(scratch),
        compiler_params=pltpu.CompilerParams(vmem_limit_bytes=VMEM_LIMIT),
        cost_estimate=pl.CostEstimate(
            flops=flops, bytes_accessed=bytes_accessed, transcendentals=transcendentals
        ),
        name=name,
    )(*args)


def slot_masks(labels, own_count, slots):
    live = slots < own_count
    return (live & (labels == 0)).astype(jnp.float32), (live & (labels != 0)).astype(jnp.float32)


def counts_kernel(here_ref, counts_ref, labels_ref, *refs):
    out_ref = refs[-1]
    own_count = counts_ref[here_ref[0]]
    shape = labels_ref.shape
    slots = lax.broadcasted_iota(jnp.int32, shape, 0) * shape[1] + lax.broadcasted_iota(jnp.int32, shape, 1)
    mask_a, mask_b = slot_masks(labels_ref[...], own_count, slots)
    first = lax.broadcasted_iota(jnp.int32, out_ref.shape, 0) == 0
    out_ref[...] = jnp.where(first, jnp.sum(mask_a), jnp.sum(mask_b))


def own_counts(here, counts, labels, after):
    return call(
        counts_kernel,
        "own_counts",
        jax.ShapeDtypeStruct((8, 128), jnp.float32),
        [SMEM, SMEM, VMEM] + [ANY] * len(after),
        (here, counts, labels.reshape(-1, 128), *after),
    )


def weights_kernel(mask_a_ref, mask_b_ref, *refs):
    out = refs[-1]
    pair = refs[0][...]
    for ref in refs[1:-1]:
        pair = pair + ref[...]
    count_a, count_b = pair[0:1, 0:1], pair[1:2, 0:1]
    balance = jnp.sqrt(count_a * count_b / (count_a + count_b))
    out[...] = mask_a_ref[...] * (balance / count_a) - mask_b_ref[...] * (balance / count_b)


def row_weights(mask_a, mask_b, pairs):
    out_shape = jax.ShapeDtypeStruct(mask_a.shape, jnp.float32)
    return call(weights_kernel, "row_weights", out_shape, [VMEM] * (2 + len(pairs)), (mask_a, mask_b, *pairs))


def rows_kernel(parts, here_ref, counts_ref, x_ref, z_ref, flips_ref, labels_ref,
                held_x_ref, held_z_ref, scale_ref, signs_ref, mask_a_ref, mask_b_ref, flips_buf, x_sem, z_sem, f_sem):
    rows, width = x_ref.shape
    block = rows // parts
    tile = z_ref.shape[0] // parts

    def x_copy(i):
        here = pl.ds(i * block, block)
        return pltpu.make_async_copy(x_ref.at[here, :], held_x_ref.at[here, :], x_sem.at[i])

    def z_copy(i):
        here = pl.ds(i * tile, tile)
        return pltpu.make_async_copy(z_ref.at[here, :], held_z_ref.at[here, :], z_sem.at[i])

    flips_copy = pltpu.make_async_copy(flips_ref, flips_buf, f_sem)
    for i in range(parts):
        x_copy(i).start()
    flips_copy.start()
    for i in range(parts):
        z_copy(i).start()
    own_count = counts_ref[here_ref[0]]
    for j in range(rows // 128):
        here = pl.ds(j * 128, 128)
        labels = jnp.transpose(jnp.broadcast_to(labels_ref[pl.ds(j, 1), :], (128, 128)))[:, 0:1]
        slots = j * 128 + lax.broadcasted_iota(jnp.int32, (128, 1), 0)
        mask_a_ref[here, :], mask_b_ref[here, :] = slot_masks(labels, own_count, slots)
    for i in range(parts):
        x_copy(i).wait()
        here = pl.ds(i * block, block)
        x = held_x_ref[here, :].astype(jnp.float32)
        mean = jnp.sum(x * x, axis=1, keepdims=True) * (1.0 / width)
        scale_ref[here, :] = lax.rsqrt(mean + 1e-06) * (0.5 / math.sqrt(width))
    flips_copy.wait()
    signs_ref[...] = (2 * flips_buf[...] - 1).astype(jnp.bfloat16)
    for i in range(parts):
        z_copy(i).wait()


def prepare_rows(here, counts, x, z, flips, labels):
    rows, width = x.shape
    perms = flips.shape[0]
    parts = 8
    column = jax.ShapeDtypeStruct((rows, 1), jnp.float32)
    return call(
        functools.partial(rows_kernel, parts),
        "prepare_rows",
        [
            pltpu.VMEM((rows, width), x.dtype),
            pltpu.VMEM(z.shape, z.dtype),
            column,
            jax.ShapeDtypeStruct((perms, rows), jnp.bfloat16),
            column,
            column,
        ],
        [SMEM, SMEM, HBM, HBM, HBM, VMEM],
        (here, counts, in_hbm(x), in_hbm(z), in_hbm(flips), labels.reshape(-1, 128)),
        flops=3 * rows * width,
        bytes_accessed=(rows + z.shape[0]) * width * 2 + perms * rows * 4,
        scratch=[
            pltpu.VMEM(flips.shape, flips.dtype),
            pltpu.SemaphoreType.DMA((parts,)),
            pltpu.SemaphoreType.DMA((parts,)),
            pltpu.SemaphoreType.DMA,
        ],
    )


def moments_kernel(first, x_ref, z_ref, scale_ref, signs_ref, weight_ref, *rest):
    out_ref = rest[-1]
    z = z_ref[pl.ds(first, TILE), :]
    z32 = z.astype(jnp.float32)
    mean = jnp.sum(z32 * z32, axis=1, keepdims=True) * (1.0 / z.shape[1])
    point = jnp.broadcast_to(lax.rsqrt(mean + 1e-06), (TILE, 128))
    point_row = jnp.transpose(point)[0:1, :]
    cross = lax.dot_general(x_ref[...], z, NT, preferred_element_type=jnp.float32)
    kern = jnp.exp(cross * scale_ref[...] * point_row)
    weighted = (weight_ref[...] * kern).astype(jnp.bfloat16)
    out_ref[...] = jnp.dot(signs_ref[...], weighted, preferred_element_type=jnp.float32).astype(jnp.bfloat16)


def moments_part(first, x, z, scale, signs, weight, after):
    rows, width = x.shape
    perms = signs.shape[0]
    return call(
        functools.partial(moments_kernel, first),
        "moments",
        jax.ShapeDtypeStruct((perms, TILE), jnp.bfloat16),
        [VMEM] * 5 + [ANY] * len(after),
        (x, z, scale, signs, weight, *after),
        flops=2 * rows * width * TILE + 2 * perms * rows * TILE,
        bytes_accessed=TILE * width * 2,
        transcendentals=rows * TILE,
    )


def load_kernel(factor_ref, *refs):
    held_ref, sem = refs[-2:]
    parts = sem.shape[0]
    block = factor_ref.shape[0] // parts
    copies = []
    for i in range(parts):
        here = pl.ds(i * block, block)
        copies.append(pltpu.make_async_copy(factor_ref.at[here, :], held_ref.at[here, :], sem.at[i]))
        copies[-1].start()
    for copy in copies:
        copy.wait()


def load_factor(factor, after):
    return call(
        load_kernel,
        "load_factor",
        pltpu.VMEM(factor.shape, factor.dtype),
        [HBM] + [ANY] * len(after),
        (in_hbm(factor), *after),
        bytes_accessed=factor.size * 2,
        scratch=[pltpu.SemaphoreType.DMA((8,))],
    )


def whiten_kernel(table, count, first, spot_ref, factor_ref, *refs):
    out, parts = refs[-1], refs[:count]
    moments = jnp.concatenate([part[...] for part in parts], axis=1)
    rows = pl.ds(first, moments.shape[1])
    wide = out.shape[2]
    spot = spot_ref[0]
    for i, (zero, one) in enumerate(table):
        block = jnp.bitwise_xor(jnp.where(spot % 2 == 0, zero, one), spot)
        here = pl.ds(pl.multiple_of(block * wide, wide), wide)
        value = jnp.dot(moments, factor_ref[rows, here], preferred_element_type=jnp.float32)
        if first > 0:
            value = value + refs[count][i]
        out[i] = value.astype(out.dtype)


def whiten(table, spot, factor, parts, blocks, after=(), partial=None):
    depth, columns = factor.shape
    perms, piece = parts[0].shape
    wide = columns // blocks
    given = [] if partial is None else [partial]
    first = 0 if partial is None else depth - len(parts) * piece
    return call(
        functools.partial(whiten_kernel, table, len(parts), first),
        "whiten_first" if partial is None else "whiten",
        jax.ShapeDtypeStruct((len(table), perms, wide), jnp.float32 if partial is None else jnp.bfloat16),
        [SMEM] + [VMEM] * (1 + len(parts) + len(given)) + [ANY] * len(after),
        (spot, factor, *parts, *given, *after),
        flops=2 * perms * len(parts) * piece * wide * len(table),
        bytes_accessed=len(parts) * piece * wide * len(table) * 2,
    )


def add_kernel(a_ref, b_ref, *outs):
    at = 0
    for out in outs:
        here = pl.ds(at, out.shape[0])
        out[...] = add(a_ref[here], b_ref[here])
        at += out.shape[0]


def add_blocks(a, b, counts):
    outs = [jax.ShapeDtypeStruct((count,) + a.shape[1:], a.dtype) for count in counts]
    return call(add_kernel, "add_blocks", outs, [VMEM, VMEM], (a, b), bytes_accessed=6 * a.size)


def finish_kernel(a_ref, b_ref, out_ref, share_ref):
    wide = jnp.transpose(a_ref[...].astype(jnp.float32) + b_ref[...].astype(jnp.float32))
    out_ref[...] = wide.astype(jnp.bfloat16)
    share = jnp.sum(wide * wide, axis=0, keepdims=True)
    for j in range(share_ref.shape[1]):
        row = share[:, j * 128:(j + 1) * 128]
        share_ref[:, j, :] = jnp.broadcast_to(row, (share_ref.shape[0], 128))


def finish(a, b, copies):
    perms, wide = a.shape
    return call(
        finish_kernel,
        "finish",
        [
            jax.ShapeDtypeStruct((wide, perms), jnp.bfloat16),
            jax.ShapeDtypeStruct((copies, perms // 128, 128), jnp.float32),
        ],
        [VMEM, VMEM],
        (a, b),
        flops=4 * perms * wide,
        bytes_accessed=perms * wide * 6,
    )


def add(a, b):
    return (a.astype(jnp.float32) + b.astype(jnp.float32)).astype(jnp.bfloat16)


def each_place(place, options, body):
    low, high = options[0], options[-1]
    for r in options:
        if low == high:
            body(r)
        elif r == low:
            pl.when(place <= r)(functools.partial(body, r))
        elif r == high:
            pl.when(place >= r)(functools.partial(body, r))
        else:
            pl.when(place == r)(functools.partial(body, r))


def sum_kernel(terms, depth_ref, *refs):
    out = refs[-1]

    def body(d):
        first, *rest = terms[d]
        if not rest:
            out[...] = refs[first][...]
            return
        value = refs[first][...].astype(jnp.float32)
        for i in rest:
            value = value + refs[i][...].astype(jnp.float32)
        out[...] = value.astype(out.dtype)

    each_place(depth_ref[0], sorted(terms), body)


def sum_at(name, depth, options, after=()):
    args = []
    for arrays in options.values():
        args += [a for a in arrays if not any(a is b for b in args)]
    place = lambda a: next(i for i, b in enumerate(args) if a is b)
    terms = {d: [place(a) for a in arrays] for d, arrays in options.items()}
    return call(
        functools.partial(sum_kernel, terms),
        name,
        jax.ShapeDtypeStruct(args[0].shape, args[0].dtype),
        [SMEM] + [VMEM] * len(args) + [ANY] * len(after),
        (depth, *args, *after),
        bytes_accessed=8 * args[0].size,
    )


class SampleSum:
    def __init__(self, n, depth):
        self.n, self.depth, self.last = n, depth, n // 2 - 1
        self.pieces, self.sent, self.recv = [], {}, {}

    def has(self, c):
        return 0 <= c < len(self.pieces)

    def inner(self, d, c):
        return [self.pieces[c]] + ([self.recv[(d - 1) % 2, c + d - 1]] if d > 0 else [])

    def whole(self, d, c):
        if d == self.last:
            key = (d % 2, c + d)
            return [self.sent[key], self.recv[key]]
        return [self.recv[d % 2, c + self.n - 1 - d]]

    def exchange(self, parity, period, after=()):
        options = {}
        for d in range(self.last + 1):
            if d % 2 == parity:
                if self.has(period - d):
                    options[d] = self.inner(d, period - d)
            elif d > 0 and self.has(period - (self.n - d)):
                options[d] = self.whole(d, period - (self.n - d))
        if not options:
            return None
        value = sum_at("exchanged", self.depth, options, after)
        pairs = []
        for i in range(parity, self.n - 1, 2):
            pairs += [(i, i + 1), (i + 1, i)]
        self.sent[parity, period] = value
        self.recv[parity, period] = lax.ppermute(value, "sample", pairs)
        return value

    def total(self, c, after=()):
        return sum_at("total", self.depth, {d: self.whole(d, c) for d in range(self.last + 1)}, after)


def make_local(mesh):
    n_sample = mesh.shape["sample"]
    n_landmark = mesh.shape["landmark"]
    n_all = n_sample * n_landmark
    bits = n_landmark.bit_length() - 1
    siblings = [(m, m ^ 1) for m in range(n_landmark)]

    def order_of(core):
        rest = list(range(1, bits))
        return [0] + (rest if core == 0 else rest[::-1])

    def place_of(core, q):
        return sum(((q >> t) & 1) << bit for t, bit in enumerate(order_of(core)))

    def local(embeddings, landmarks, factor, flips, labels, counts):
        here = lax.axis_index("sample").astype(jnp.int32)
        spot = lax.axis_index("landmark").astype(jnp.int32)
        depth = jnp.minimum(here, n_sample - 1 - here).reshape(1)
        here, spot = here.reshape(1), spot.reshape(1)
        points = landmarks.shape[0]
        perms = flips.shape[0]
        count = points // TILE

        kept_places = [2 * q for q in range(n_landmark // 2)]
        kept_order = sorted(kept_places, key=lambda q: [-((q >> t) & 1) for t in range(1, bits)])
        sent_order = [q + 1 for q in kept_order]

        def table_of(places, swapped):
            cores = (1, 0) if swapped else (0, 1)
            return [tuple(place_of(core, q) for core in cores) for q in places]

        def pairs_of(t):
            return [(m, m ^ (1 << order_of(m % 2)[t])) for m in range(n_landmark)]

        own_pair = own_counts(here, counts, labels, [depth, spot])
        pairs = [own_pair]
        for shift in range(1, n_sample):
            to = [(i, (i + shift) % n_sample) for i in range(n_sample)]
            pairs.append(lax.ppermute(own_pair, "sample", to))
        x, z, scale, signs, mask_a, mask_b = prepare_rows(here, counts, embeddings, landmarks, flips, labels)
        weight = row_weights(mask_a, mask_b, pairs)

        line = SampleSum(n_sample, depth)
        totals = []
        value = None
        for t in range(count + n_sample - 1):
            if t < count:
                after = [value] if t > 0 else []
                after += [line.recv[1, t - 2]] if (1, t - 2) in line.recv else []
                line.pieces.append(moments_part(t * TILE, x, z, scale, signs, weight, after))
            after = totals[-1:] + line.pieces[-1:]
            if t == count:
                held_factor = load_factor(factor, [value, line.recv[1, t - 2]])
                after.append(held_factor)
            for parity in (1, 0):
                sent = line.exchange(parity, t, after)
                if sent is not None:
                    value, after = sent, [sent]
            if t >= n_sample:
                totals.append(line.total(t - n_sample))
        middle = len(kept_order) // 2
        tables = []
        for part in (slice(0, middle), slice(middle, None)):
            tables += [table_of(sent_order[part], True), table_of(kept_order[part], False)]
        firsts = [whiten(table, spot, held_factor, totals[:count // 2], n_landmark) for table in tables]
        totals.append(line.total(count - 1, firsts[:3]))
        late = totals[count // 2:]
        sums = []
        for i in (0, 2):
            sent = whiten(tables[i], spot, held_factor, late, n_landmark, sums[-1:], firsts[i])
            recv = lax.ppermute(sent, "landmark", siblings)
            kept = whiten(tables[i + 1], spot, held_factor, late, n_landmark, [sent], firsts[i + 1])
            (total,) = add_blocks(kept, recv, [kept.shape[0]])
            sums.append(total)
        recv = lax.ppermute(sums[0], "landmark", pairs_of(1))
        kept = sums[1]
        for t in range(2, bits):
            half = kept.shape[0] // 2
            sent, kept = add_blocks(kept, recv, [half, half])
            recv = lax.ppermute(sent, "landmark", pairs_of(t))
        whitened, share = finish(kept[0], recv[0], n_all)
        share = lax.all_to_all(share, ("sample", "landmark"), 0, 0, tiled=True)
        statistic = jnp.sum(share, axis=0).reshape(perms)
        return whitened, statistic / (points * n_landmark)

    return local


def solution(mesh):
    return jax.shard_map(
        make_local(mesh),
        mesh=mesh,
        in_specs=(
            P("sample", None),
            P("landmark", None),
            P("landmark", "sample"),
            P(None, "sample"),
            P("sample"),
            P(),
        ),
        out_specs=(P(("sample", "landmark"), None), P()),
        check_vma=False,
    )
```
